512 devices in a mesh: dp: 32 (over y, x_lo, core), ctx: 16 (over z, x_hi).
Axes of the slice: x: 4 (x_hi: 2, x_lo: 2; x = x_hi * 2 + x_lo), y: 8, z: 8, core: 2. Of those that a mesh axis runs over, the one named last changes fastest.
Arguments:
- frames: bfloat16 [98304, 1536], P(('dp', 'ctx')), may hold values from -48 to 48
- seg_ids: int32 [32, 3072], P('dp'), may hold values from 0 to 7, never falling along the last dimension, each value on 1 to 768 neighbouring positions
- assign: int32 [32, 16], P('dp'), may hold values from 0 to 15, each once within a row
- w_qkv: bfloat16 [3, 1536, 1536], P(None, 'dp', 'ctx'), may hold values from -1 to 1
Outputs:
- context: bfloat16 [98304, 1536], P(('dp', 'ctx'))
The draws below stay inside these ranges and needn't reach their ends.
Inputs may be any that keep to these rules, and one draw needn't show every extreme that they name: `seg_ids`: never falls along a sequence; each utterance has 1 to 768 frames, one exactly 768. `assign`: each row is a permutation.
All inputs are finite; a program needn't handle non-finite values.
Results may differ from the reference program's by a relative error of at most 0.0073.
Values may be sent and summed in bfloat16 or wider, within the bound.
No kernel may reach another device: no remote copies, remote signals or barrier semaphores. Data moves between devices by JAX's collectives and lax.ppermute only.
A program may use at most 64 MiB of HBM per device.

```python
import math
import jax
import jax.numpy as jnp
import numpy as np
from jax import lax

HEADS = 16
HEAD = 96
D = 1536
FR_DEV = 192
UTTS = 8
SEQ = 3072
MOST = 768
GROUPS = 32
FRAMES = 98304
BLOCK = 512
N_CTX = 16


def draw_frames(key, part):
    key = jax.random.fold_in(key, 5)
    first = jax.random.fold_in(key, 0)
    base = jnp.clip(jax.random.normal(first, (FRAMES, D), jnp.float32), -6.0, 6.0)
    return base.astype(jnp.bfloat16)


def draw_w_qkv(key, part):
    key = jax.random.fold_in(key, 7)
    first, second, third = jax.random.split(key, 3)
    query_part = jnp.clip(jax.random.normal(first, (D, D), jnp.float32), -6.0, 6.0)
    key_part = jnp.clip(jax.random.normal(second, (D, D), jnp.float32), -6.0, 6.0)
    value_part = jnp.clip(jax.random.normal(third, (D, D), jnp.float32), -6.0, 6.0)
    stacked = jnp.stack([query_part, key_part, value_part], axis=0) * D ** (-0.5)
    return stacked.astype(jnp.bfloat16)


def split_up(number_of, total, bound, lean):
    loads = [(1 << 20) // math.isqrt(grade ** lean) + 1 for grade in range(2, number_of + 1)]
    surplus, given = total - bound - (number_of - 1), [1] * (number_of - 1)
    while surplus > 0:
        movable = [i for i in range(number_of - 1) if given[i] < bound]
        mass, budget = sum([loads[i] for i in movable]), surplus
        for i in movable:
            extra = min(bound - given[i], max(1, budget * loads[i] // mass), surplus)
            given[i] = given[i] + extra
            surplus = surplus - extra
    return np.array([bound] + given)


def ragged(stream_key, number_of, total, most, slope):
    if number_of == 2:
        one = jax.random.randint(stream_key, (), max(1, total - most), min(most, total - 1) + 1)
        return jnp.stack([one, total - one])
    tallies = jnp.asarray(split_up(number_of, total, most, slope), jnp.int32)
    twos = (number_of - 1) // 2
    source_of, receiver = tallies[1:1 + 2 * twos:2], tallies[2:2 + 2 * twos:2]
    margin = jnp.minimum(source_of - 1, most - receiver)
    shifted = jax.random.randint(jax.random.fold_in(stream_key, 1), (twos,), 0, 1 << 20) % (margin + 1)
    tallies = tallies.at[1:1 + 2 * twos:2].set(source_of - shifted).at[2:2 + 2 * twos:2].set(receiver + shifted)
    return tallies[jax.random.permutation(jax.random.fold_in(stream_key, 2), number_of)]


def setup_inputs(seed: int = 0) -> dict:
    streams_of = jax.random.split(jax.random.key(seed), 5)
    return {
        "frames": draw_frames(jax.random.fold_in(streams_of[4], 71), 0),
        "seg_ids": jax.vmap(lambda own: jnp.searchsorted(jnp.cumsum(ragged(own, UTTS, SEQ, MOST, 0)), jnp.arange(SEQ), side="right"))(jax.random.split(streams_of[1], GROUPS)).reshape((GROUPS, SEQ)).astype(jnp.int32),
        "assign": jax.vmap(lambda own: jax.random.permutation(own, N_CTX))(jax.random.split(streams_of[2], GROUPS)).reshape((GROUPS, N_CTX)).astype(jnp.int32),
        "w_qkv": draw_w_qkv(jax.random.fold_in(streams_of[4], 71), 0),
    }


def attend_all(queries, keys, values, ids, block):
    scale = queries.shape[-1] ** -0.5
    count = queries.shape[0] // block

    def one(index):
        qblock = lax.dynamic_slice_in_dim(queries, index * block, block, 0)
        qids = lax.dynamic_slice_in_dim(ids, index * block, block, 0)
        scores = jnp.dot(qblock, keys.T, preferred_element_type=jnp.float32) * scale
        scores = jnp.where(qids[:, None] == ids[None, :], scores, -1e30)
        top = jnp.max(scores, axis=1, keepdims=True)
        expo = jnp.exp(scores - top)
        weights = (expo / jnp.sum(expo, axis=1, keepdims=True)).astype(jnp.bfloat16)
        return jnp.dot(weights, values, preferred_element_type=jnp.float32).astype(jnp.bfloat16)

    result = lax.map(one, jnp.arange(count, dtype=jnp.int32))
    return result.reshape(queries.shape[0], queries.shape[1])


def reference(frames, seg_ids, assign, w_qkv):
    def group(index):
        rows = lax.dynamic_slice_in_dim(frames, index * SEQ, SEQ, 0)
        ids = lax.dynamic_index_in_dim(seg_ids, index, 0, keepdims=False)
        order = lax.dynamic_index_in_dim(assign, index, 0, keepdims=False)
        store_ids = jnp.take(ids.reshape(N_CTX, FR_DEV), order, axis=0).reshape(SEQ)
        queries = jnp.dot(rows, w_qkv[0], preferred_element_type=jnp.float32).astype(jnp.bfloat16)
        keys = jnp.dot(rows, w_qkv[1], preferred_element_type=jnp.float32).astype(jnp.bfloat16)
        values = jnp.dot(rows, w_qkv[2], preferred_element_type=jnp.float32).astype(jnp.bfloat16)

        def split_heads(array):
            return array.reshape(SEQ, HEADS, HEAD).transpose(1, 0, 2)

        def per_head(triple):
            return attend_all(triple[0], triple[1], triple[2], store_ids, BLOCK)

        heads_out = lax.map(per_head, (split_heads(queries), split_heads(keys), split_heads(values)))
        return heads_out.transpose(1, 0, 2).reshape(SEQ, D)

    result = lax.map(group, jnp.arange(GROUPS, dtype=jnp.int32))
    return result.reshape(FRAMES, D)
```

```python
import functools

import jax
import jax.numpy as jnp
from jax import lax
from jax.experimental import pallas as pl
from jax.experimental.pallas import tpu as pltpu
from jax.sharding import Mesh
from jax.sharding import PartitionSpec as P

HEAD = 96
FR = 192
D = 1536
NZ = 8
SEQ = 3072
TILE = 256
MAX_TILES = 8
ROWS = NZ * FR
AXES = ("y", "xl", "core", "z", "xh")
SIZES = (8, 2, 2, 8, 2)


def swap(x, axis):
    return lax.ppermute(x, axis, [(0, 1), (1, 0)])


def both(own, other, index, axis):
    first = jnp.where(index == 0, own, other)
    second = jnp.where(index == 0, other, own)
    return jnp.stack([first, second], axis=axis)


def gather_weights(w):
    xh = lax.axis_index("xh")
    flat = jnp.transpose(w, (1, 0, 2)).reshape(w.shape[1], 3 * HEAD)
    heads = both(flat, swap(flat, "xh"), xh, 0)
    q, k, v = (heads[:, :, t * HEAD : (t + 1) * HEAD] for t in range(3))
    shard = jnp.concatenate([jnp.zeros_like(q[0, :, :64]), q[0], q[1], v[0], v[1], k[0], k[1]], axis=1)
    rows = lax.all_to_all(jnp.broadcast_to(shard[None], (8,) + shard.shape), "y", 0, 0, tiled=True)
    rows = both(rows, swap(rows, "xl"), lax.axis_index("xl"), 1)
    rows = both(rows, swap(rows, "core"), lax.axis_index("core"), 2)
    return rows.reshape(D, shard.shape[1])


def project_kernel(x_ref, w_ref, kv_ref, q_ref):
    x = x_ref[...]
    kv_ref[...] = jnp.dot(x, w_ref[:, 256:], preferred_element_type=jnp.float32).astype(jnp.bfloat16)
    q_ref[...] = jnp.dot(x, w_ref[:, :256], preferred_element_type=jnp.float32).astype(jnp.bfloat16)


def project(x, w):
    step = 256
    n = x.shape[0]
    return pl.pallas_call(
        project_kernel,
        grid=(n // step,),
        in_specs=[pl.BlockSpec((step, D), lambda i: (i, 0)), pl.BlockSpec((D, 640), lambda i: (0, 0))],
        out_specs=[pl.BlockSpec((step, 384), lambda i: (i, 0)), pl.BlockSpec((step, 256), lambda i: (i, 0))],
        out_shape=[jax.ShapeDtypeStruct((n, 384), jnp.bfloat16), jax.ShapeDtypeStruct((n, 256), jnp.bfloat16)],
        compiler_params=pltpu.CompilerParams(vmem_limit_bytes=24 << 20),
        cost_estimate=pl.CostEstimate(flops=2 * n * D * 640, bytes_accessed=2 * (n * D + D * 640 + n * 640), transcendentals=0),
    )(x, w)


def attend_kernel(info_ref, own_ref, other_ref, q_ref, qid_ref, kid_ref, out_ref, kv_ref, s_ref):
    xh = info_ref[32]
    kv_ref[SEQ:, :] = jnp.zeros((TILE, 384), jnp.bfloat16)
    for z in range(NZ):
        for ref, side in ((own_ref, xh), (other_ref, 1 - xh)):
            at = pl.multiple_of(info_ref[2 * z + side] * FR, FR)
            kv_ref[pl.ds(at, FR), :] = ref[z * FR : (z + 1) * FR, :]
    scale = HEAD**-0.5 * 1.4426950408889634
    lane = lax.broadcasted_iota(jnp.int32, (FR, 256), 1)

    def block(z, _):
        rows = pl.ds(pl.multiple_of(z * FR, FR), FR)
        q = q_ref[rows, :]
        zero = jnp.zeros_like(q)
        q2 = jnp.concatenate([jnp.where(lane < 160, q, zero), jnp.where(lane >= 160, q, zero)], axis=0)
        qid = qid_ref[rows, :]
        qid2 = jnp.concatenate([qid, qid], axis=0)
        first, count = info_ref[16 + z], info_ref[24 + z]

        def score(t, top):
            at = pl.multiple_of(first + t * TILE, 128)
            keys = kv_ref[pl.ds(at, TILE), 128:384]
            s = lax.dot_general(q2, keys, (((1,), (1,)), ((), ())), preferred_element_type=jnp.float32)
            s = jnp.where(qid2 == kid_ref[:, pl.ds(at, TILE)], s, -1e30)
            s_ref[t] = s
            return jnp.maximum(top, jnp.maximum(s[:, :128], s[:, 128:]))

        top = lax.fori_loop(0, count, score, jnp.full((2 * FR, 128), -1e30, jnp.float32))
        top = jnp.max(top, axis=1, keepdims=True)

        def weigh(t, carry):
            total, acc = carry
            at = pl.multiple_of(first + t * TILE, 128)
            p = jnp.exp2((s_ref[t] - top) * scale)
            total = total + (p[:, :128] + p[:, 128:])
            acc = acc + jnp.dot(p.astype(jnp.bfloat16), kv_ref[pl.ds(at, TILE), :256], preferred_element_type=jnp.float32)
            return total, acc

        total, acc = lax.fori_loop(
            0, count, weigh, (jnp.zeros((2 * FR, 128), jnp.float32), jnp.zeros((2 * FR, 256), jnp.float32))
        )
        acc = acc / jnp.sum(total, axis=1, keepdims=True)
        o = jnp.where(lane < HEAD, acc[:FR], acc[FR:])
        tail = o[:, 128:]
        half = lax.broadcasted_iota(jnp.int32, (FR // 2, 128), 1) < 64
        packed = jnp.where(half, tail[: FR // 2], pltpu.roll(tail[FR // 2 :], 64, 1))
        out_ref[z, :FR, :] = o[:, :128].astype(jnp.bfloat16)
        out_ref[z, FR:, :] = packed.astype(jnp.bfloat16)
        return 0

    lax.fori_loop(0, NZ, block, 0)


def attend(info, own, other, q, qid, kid):
    vmem = pl.BlockSpec(memory_space=pltpu.VMEM)
    return pl.pallas_call(
        attend_kernel,
        in_specs=[pl.BlockSpec(memory_space=pltpu.SMEM)] + [vmem] * 5,
        out_specs=vmem,
        out_shape=jax.ShapeDtypeStruct((NZ, FR * 3 // 2, 128), jnp.bfloat16),
        scratch_shapes=[
            pltpu.VMEM((SEQ + TILE, 384), jnp.bfloat16),
            pltpu.VMEM((MAX_TILES, 2 * FR, TILE), jnp.float32),
        ],
        compiler_params=pltpu.CompilerParams(vmem_limit_bytes=40 << 20),
        cost_estimate=pl.CostEstimate(flops=8 << 30, bytes_accessed=8 << 20, transcendentals=4 << 20),
    )(info, own, other, q, qid, kid)


def unpack_kernel(in_ref, out_ref):
    half = lax.broadcasted_iota(jnp.int32, (FR, 128), 1) < 64
    for z in range(0, NZ, 2):
        tails = []
        for i in (z, z + 1):
            packed = in_ref[i, FR:, :].astype(jnp.float32)
            tails.append(jnp.concatenate([packed, pltpu.roll(packed, 64, 1)], axis=0))
        second = pltpu.roll(in_ref[z + 1, :FR, :].astype(jnp.float32), 64, 1)
        out_ref[:, z * 192 : z * 192 + 128] = in_ref[z, :FR, :]
        out_ref[:, z * 192 + 128 : z * 192 + 256] = jnp.where(half, tails[0], second).astype(jnp.bfloat16)
        out_ref[:, z * 192 + 256 : z * 192 + 384] = jnp.where(half, second, pltpu.roll(tails[1], 64, 1)).astype(jnp.bfloat16)


def unpack(packed):
    vmem = pl.BlockSpec(memory_space=pltpu.VMEM)
    return pl.pallas_call(
        unpack_kernel,
        in_specs=[vmem],
        out_specs=vmem,
        out_shape=jax.ShapeDtypeStruct((FR, D), jnp.bfloat16),
        compiler_params=pltpu.CompilerParams(vmem_limit_bytes=8 << 20),
    )(packed)


def plan(ids, order, xh):
    blocks = ids.reshape(16, FR)
    own = lax.dynamic_index_in_dim(order.reshape(NZ, 2), xh, 1, keepdims=False)
    qid = jnp.take(blocks, own, axis=0)
    first = jnp.sum(ids[None, :] < qid[:, :1], axis=1, dtype=jnp.int32)
    last = jnp.sum(ids[None, :] <= qid[:, FR - 1 :], axis=1, dtype=jnp.int32)
    first = first // 128 * 128
    info = jnp.concatenate([order, first, (last - first + TILE - 1) // TILE, xh.astype(jnp.int32)[None]])
    kid = jnp.concatenate([ids, jnp.full((TILE,), -1, jnp.int32)])[None]
    return info, qid.reshape(ROWS, 1), kid


def body(frames, seg_ids, assign, w_qkv):
    xh = lax.axis_index("xh")
    x = lax.all_gather(frames, "z", axis=0, tiled=True)
    info, qid, kid = plan(seg_ids[0], assign[0], xh)
    kv, q = project(x, gather_weights(w_qkv))
    packed = attend(info, kv, swap(kv, "xh"), q, qid, kid)
    return unpack(lax.all_to_all(packed, "z", 0, 0, tiled=True))


def solution(mesh):
    fine = Mesh(mesh.devices.reshape(SIZES), AXES)
    dp, ctx = AXES[:3], AXES[3:]
    return jax.shard_map(
        body,
        mesh=fine,
        in_specs=(P(AXES, None), P(dp, None), P(dp, None), P(None, dp, ctx)),
        out_specs=P(AXES, None),
        check_vma=False,
    )
```

```python
import functools

import jax
import jax.numpy as jnp
from jax import lax
from jax.experimental import pallas as pl
from jax.experimental.pallas import tpu as pltpu
from jax.sharding import Mesh
from jax.sharding import PartitionSpec as P

HEAD = 96
FR = 192
D = 1536
NZ = 8
SEQ = 3072
TILE = 256
MAX_TILES = 8
PAD = SEQ + TILE
AXES = ("y", "xl", "core", "z", "xh")
SIZES = (8, 2, 2, 8, 2)
SLOTS = (0, -1, 1, -2, 2, -3, 3, 4)
EARLY = 3
LATE = 7
WIDE = 704
VMEM = pl.BlockSpec(memory_space=pltpu.VMEM)
SMEM = pl.BlockSpec(memory_space=pltpu.SMEM)


def swap(x, axis):
    return lax.ppermute(x, axis, [(0, 1), (1, 0)])


def shift(x, by):
    return lax.ppermute(x, "z", [(i, (i - by) % NZ) for i in range(NZ)])


def both(own, other, index, axis):
    first = jnp.where(index == 0, own, other)
    second = jnp.where(index == 0, other, own)
    return jnp.stack([first, second], axis=axis)


def near_weights(w):
    flat = jnp.transpose(w, (1, 0, 2)).reshape(w.shape[1], 3 * HEAD)
    heads = both(flat, swap(flat, "xh"), lax.axis_index("xh"), 0)
    q, k, v = (heads[:, :, t * HEAD : (t + 1) * HEAD] for t in range(3))
    zero = jnp.zeros_like(q[0, :, :64])
    shard = jnp.concatenate([zero, q[0], q[1], v[0], v[1], k[0], k[1], zero], axis=1)
    return both(shard, swap(shard, "xl"), lax.axis_index("xl"), 0).reshape(96, WIDE)


def project_body(core_ref, wa_ref, wb_ref, own_refs, partner_refs, kv_ref, q_ref, part_ref, w_ref):
    core = core_ref[0]
    for i in range(16):
        for ref, side in ((wa_ref, core), (wb_ref, 1 - core)):
            at = pl.multiple_of(i * 96 + side * 48, 16)
            w_ref[pl.ds(at, 48), :] = ref[i * 48 : (i + 1) * 48, :640]
    if partner_refs:
        x = jnp.concatenate([r[...] for r in partner_refs], axis=0)
        part_ref[...] = jnp.dot(x, w_ref[:, 256:], preferred_element_type=jnp.float32).astype(jnp.bfloat16)
    x = jnp.concatenate([r[...] for r in own_refs], axis=0)
    kv_ref[...] = jnp.dot(x, w_ref[:, 256:], preferred_element_type=jnp.float32).astype(jnp.bfloat16)
    q_ref[...] = jnp.dot(x, w_ref[:, :256], preferred_element_type=jnp.float32).astype(jnp.bfloat16)


def project(core, wa, wb, own, partner):
    n, m = len(own), len(partner)

    def kernel(core_ref, wa_ref, wb_ref, *refs):
        outs = refs[n + m :]
        part_ref = outs[2] if m else None
        project_body(core_ref, wa_ref, wb_ref, refs[:n], refs[n : n + m], outs[0], outs[1], part_ref, outs[-1])

    shapes = [(n * FR, 384), (n * FR, 256)] + ([(m * FR, 384)] if m else [])
    return pl.pallas_call(
        kernel,
        in_specs=[SMEM] + [VMEM] * (2 + n + m),
        out_specs=[VMEM] * len(shapes),
        out_shape=[jax.ShapeDtypeStruct(s, jnp.bfloat16) for s in shapes],
        scratch_shapes=[pltpu.VMEM((D, 640), jnp.bfloat16)],
        compiler_params=pltpu.CompilerParams(vmem_limit_bytes=32 << 20),
        cost_estimate=pl.CostEstimate(flops=2 * (n + m) * FR * D * 640, bytes_accessed=4 << 20, transcendentals=0),
    )(core, wa, wb, *own, *partner)


def attend_kernel(info_ref, qid_ref, kid_ref, kva, kvb, qa, qb, part, kvra, kvrb, out_ref, kv_ref, q_ref):
    kv_ref[SEQ:, :] = jnp.zeros((TILE, 384), jnp.bfloat16)
    for s in range(NZ):
        own, i = (kva, s) if s < LATE else (kvb, s - LATE)
        kv_ref[pl.ds(pl.multiple_of(info_ref[s] * FR, FR), FR), :] = own[i * FR : (i + 1) * FR, :]
        if s < EARLY:
            other, i = part, s
        else:
            other, i = (kvra, s - EARLY) if s < LATE else (kvrb, s - LATE)
        kv_ref[pl.ds(pl.multiple_of(info_ref[8 + s] * FR, FR), FR), :] = other[i * FR : (i + 1) * FR, :]
    q_ref[: LATE * FR, :] = qa[...]
    q_ref[LATE * FR :, :] = qb[...]
    scale = HEAD**-0.5 * 1.4426950408889634
    lane = lax.broadcasted_iota(jnp.int32, (FR, 256), 1)
    half = lax.broadcasted_iota(jnp.int32, (FR // 2, 128), 1) < 64

    def attend_jobs(jobs, n):
        scores, tops, outs = [], [], []
        for q, qid, first in jobs:
            tiles, top = [], None
            for t in range(n):
                at = pl.multiple_of(first + t * TILE, 128)
                s = lax.dot_general(
                    q, kv_ref[pl.ds(at, TILE), 128:], (((1,), (1,)), ((), ())), preferred_element_type=jnp.float32
                )
                s = jnp.where(qid == kid_ref[:, pl.ds(at, TILE)], s, -1e30)
                tiles.append(s)
                most = jnp.maximum(s[:, :128], s[:, 128:])
                top = most if top is None else jnp.maximum(top, most)
            scores.append(tiles)
            tops.append(jnp.max(top, axis=1, keepdims=True))
        for (q, qid, first), tiles, top in zip(jobs, scores, tops):
            total = acc = None
            for t in range(n):
                at = pl.multiple_of(first + t * TILE, 128)
                p = jnp.exp2((tiles[t] - top) * scale)
                part_sum = p[:, :128] + p[:, 128:]
                out = jnp.dot(p.astype(jnp.bfloat16), kv_ref[pl.ds(at, TILE), :256], preferred_element_type=jnp.float32)
                total = part_sum if total is None else total + part_sum
                acc = out if acc is None else acc + out
            outs.append(acc * (1.0 / jnp.sum(total, axis=1, keepdims=True)))
        return outs

    def pair(g, _):
        slots = [info_ref[32 + 2 * g + i] for i in range(2)]
        count = info_ref[24 + slots[1]]
        jobs = []
        for s in slots:
            rows = pl.ds(pl.multiple_of(s * FR, FR), FR)
            q = q_ref[rows, :]
            zero = jnp.zeros_like(q)
            first = jnp.minimum(info_ref[16 + s], PAD - count * TILE)
            for head in (lane < 160, lane >= 160):
                jobs.append((jnp.where(head, q, zero), qid_ref[rows, :], first))

        def attend_pair(n):
            outs = attend_jobs(jobs, n)
            for i, s in enumerate(slots):
                z = info_ref[40 + s]
                o = jnp.where(lane < HEAD, outs[2 * i], outs[2 * i + 1])
                tail = o[:, 128:]
                out_ref[z, :FR, :] = o[:, :128].astype(jnp.bfloat16)
                packed = jnp.where(half, tail[: FR // 2], pltpu.roll(tail[FR // 2 :], 64, 1))
                out_ref[z, FR:, :] = packed.astype(jnp.bfloat16)

        for n in range(1, MAX_TILES + 1):
            pl.when(count == n)(functools.partial(attend_pair, n))
        return 0

    lax.fori_loop(0, NZ // 2, pair, 0)


def attend(*args):
    return pl.pallas_call(
        attend_kernel,
        in_specs=[SMEM] + [VMEM] * (len(args) - 1),
        out_specs=VMEM,
        out_shape=jax.ShapeDtypeStruct((NZ, FR * 3 // 2, 128), jnp.bfloat16),
        scratch_shapes=[pltpu.VMEM((PAD, 384), jnp.bfloat16), pltpu.VMEM((NZ * FR, 256), jnp.bfloat16)],
        compiler_params=pltpu.CompilerParams(vmem_limit_bytes=40 << 20),
        cost_estimate=pl.CostEstimate(flops=8 << 30, bytes_accessed=8 << 20, transcendentals=4 << 20),
    )(*args)


def unpack_kernel(in_ref, out_ref):
    half = lax.broadcasted_iota(jnp.int32, (FR, 128), 1) < 64
    for z in range(0, NZ, 2):
        tails = []
        for i in (z, z + 1):
            packed = in_ref[i, FR:, :].astype(jnp.float32)
            tails.append(jnp.concatenate([packed, pltpu.roll(packed, 64, 1)], axis=0))
        second = pltpu.roll(in_ref[z + 1, :FR, :].astype(jnp.float32), 64, 1)
        out_ref[:, z * 192 : z * 192 + 128] = in_ref[z, :FR, :]
        out_ref[:, z * 192 + 128 : z * 192 + 256] = jnp.where(half, tails[0], second).astype(jnp.bfloat16)
        out_ref[:, z * 192 + 256 : z * 192 + 384] = jnp.where(half, second, pltpu.roll(tails[1], 64, 1)).astype(jnp.bfloat16)


def unpack(packed):
    return pl.pallas_call(
        unpack_kernel,
        in_specs=[VMEM],
        out_specs=VMEM,
        out_shape=jax.ShapeDtypeStruct((FR, D), jnp.bfloat16),
        compiler_params=pltpu.CompilerParams(vmem_limit_bytes=8 << 20),
    )(packed)


def plan(ids, order, z, xh):
    blocks = ids.reshape(16, FR)
    zs = (z + jnp.asarray(SLOTS, jnp.int32)) % NZ
    places = jnp.take(order.reshape(NZ, 2), zs, axis=0)
    own = jnp.where(xh == 0, places[:, 0], places[:, 1])
    other = jnp.where(xh == 0, places[:, 1], places[:, 0])
    qid = jnp.take(blocks, own, axis=0)
    first = jnp.sum(ids[None, :] < qid[:, :1], axis=1, dtype=jnp.int32)
    last = jnp.sum(ids[None, :] <= qid[:, FR - 1 :], axis=1, dtype=jnp.int32)
    first = first // 128 * 128
    count = (last - first + TILE - 1) // TILE
    i = jnp.arange(NZ, dtype=jnp.int32)
    ahead = (count[None, :] < count[:, None]) | ((count[None, :] == count[:, None]) & (i[None, :] < i[:, None]))
    rank = jnp.sum(ahead, axis=1, dtype=jnp.int32)
    ranked = jnp.sum(jnp.where(rank[:, None] == i[None, :], i[:, None], 0), axis=0, dtype=jnp.int32)
    info = jnp.concatenate([own, other, first, count, ranked, zs])
    kid = jnp.concatenate([ids, jnp.full((TILE,), -1, jnp.int32)])[None]
    return info, qid.reshape(NZ * FR, 1), kid


def body(frames, seg_ids, assign, w_qkv):
    z, xh, core = (lax.axis_index(a) for a in ("z", "xh", "core"))
    near = near_weights(w_qkv)
    up, down, slots = frames, frames, [frames]
    for _ in range(3):
        up, down = shift(up, -1), shift(down, 1)
        slots += [up, down]
    mine = jnp.where(core == 0, up, down)
    by_core = [(c * NZ + i, c * NZ + (i + (1, -1)[c]) % NZ) for c in (0, 1) for i in range(NZ)]
    slots.append(lax.ppermute(mine, ("core", "z"), by_core))
    wa = lax.all_gather(near, "y", axis=0, tiled=True)
    wb = swap(wa, "core")
    early = [lax.optimization_barrier((slots[0], near))[0]] + slots[1:EARLY]
    partner = [swap(s, "xh") for s in early]
    info, qid, kid = plan(seg_ids[0], assign[0], z, xh)
    at = core.astype(jnp.int32)[None]
    kva, qa, part = project(at, wa, wb, slots[:LATE], partner)
    kvra = swap(kva[EARLY * FR :], "xh")
    kvb, qb = project(at, wa, wb, slots[LATE:], [])
    kvrb = swap(kvb, "xh")
    packed = attend(info, qid, kid, kva, kvb, qa, qb, part, kvra, kvrb)
    return unpack(lax.all_to_all(packed, "z", 0, 0, tiled=True))


def solution(mesh):
    fine = Mesh(mesh.devices.reshape(SIZES), AXES)
    dp, ctx = AXES[:3], AXES[3:]
    return jax.shard_map(
        body,
        mesh=fine,
        in_specs=(P(AXES, None), P(dp, None), P(dp, None), P(None, dp, ctx)),
        out_specs=P(AXES, None),
        check_vma=False,
    )
```

```python
import functools

import jax
import jax.numpy as jnp
from jax import lax
from jax.experimental import pallas as pl
from jax.experimental.pallas import tpu as pltpu
from jax.sharding import Mesh
from jax.sharding import PartitionSpec as P

HEAD = 96
FR = 192
D = 1536
NZ = 8
ROWS = NZ * FR
SEQ = 3072
TILE = 256
MAX_TILES = 8
PAD = SEQ + TILE
AXES = ("y", "xl", "core", "z", "xh")
SIZES = (8, 2, 2, 8, 2)
VMEM = pl.BlockSpec(memory_space=pltpu.VMEM)
SMEM = pl.BlockSpec(memory_space=pltpu.SMEM)


def swap(x, axis):
    return lax.ppermute(x, axis, [(0, 1), (1, 0)])


def both(own, other, index, axis):
    first = jnp.where(index == 0, own, other)
    second = jnp.where(index == 0, other, own)
    return jnp.stack([first, second], axis=axis)


def gather_weights(w):
    flat = jnp.transpose(w, (1, 0, 2)).reshape(w.shape[1], 3 * HEAD)
    heads = both(flat, swap(flat, "xh"), lax.axis_index("xh"), 0)
    q, k, v = (heads[:, :, t * HEAD : (t + 1) * HEAD] for t in range(3))
    shard = jnp.concatenate([k[0], v[0], v[1], k[1], q[0], jnp.zeros_like(q[0, :, :64]), q[1]], axis=1)
    rows = lax.all_to_all(jnp.broadcast_to(shard[None], (8,) + shard.shape), "y", 0, 0, tiled=True)
    rows = both(rows, swap(rows, "xl"), lax.axis_index("xl"), 1)
    rows = both(rows, swap(rows, "core"), lax.axis_index("core"), 2)
    return rows.reshape(D, shard.shape[1])


def low_lanes(rows, lanes, below):
    return lax.broadcasted_iota(jnp.int32, (rows, lanes), 1) < below


def project_first(x_ref, w_ref, kv_ref, wire_ref):
    kv = jnp.dot(x_ref[...], w_ref[...], preferred_element_type=jnp.float32)
    kv_ref[...] = kv.astype(jnp.bfloat16)
    half = low_lanes(FR // 2, 128, 64)
    for b in range(kv.shape[0] // FR):
        rest = kv[b * FR : (b + 1) * FR, 128:]
        wire_ref[b, :FR, :] = kv[b * FR : (b + 1) * FR, :128].astype(jnp.bfloat16)
        packed = jnp.where(half, rest[: FR // 2], pltpu.roll(rest[FR // 2 :], 64, 1))
        wire_ref[b, FR:, :] = packed.astype(jnp.bfloat16)


def project_second(x_ref, w_ref, kv_ref, last_ref, q_ref, wire_ref):
    x = x_ref[...]
    last = jnp.dot(x, w_ref[:, 256:384], preferred_element_type=jnp.float32).astype(jnp.bfloat16)
    last_ref[...] = last
    q_ref[...] = jnp.dot(x, w_ref[:, 384:], preferred_element_type=jnp.float32).astype(jnp.bfloat16)
    half = low_lanes(FR // 2, 128, 64)
    for b in range(x.shape[0] // FR):
        rest = kv_ref[b * FR : (b + 1) * FR, 128:].astype(jnp.float32)
        wire_ref[b, :FR, :] = last[b * FR : (b + 1) * FR]
        packed = jnp.where(half, pltpu.roll(rest[FR // 2 :], 64, 1), rest[: FR // 2])
        wire_ref[b, FR:, :] = packed.astype(jnp.bfloat16)


def project_call(kernel, widths, ins, specs):
    step = 2 * FR
    row = lambda width: pl.BlockSpec((step, width), lambda i: (i, 0))
    wire = pl.BlockSpec((step // FR, FR * 3 // 2, 128), lambda i: (i, 0, 0))
    return pl.pallas_call(
        kernel,
        grid=(ROWS // step,),
        in_specs=[row(D), pl.BlockSpec((D, specs[0]), lambda i: (0, 0))] + [row(s) for s in specs[1:]],
        out_specs=[row(s) for s in widths] + [wire],
        out_shape=[jax.ShapeDtypeStruct((ROWS, s), jnp.bfloat16) for s in widths]
        + [jax.ShapeDtypeStruct((NZ, FR * 3 // 2, 128), jnp.bfloat16)],
        compiler_params=pltpu.CompilerParams(vmem_limit_bytes=56 << 20),
        cost_estimate=pl.CostEstimate(flops=2 * ROWS * D * 384, bytes_accessed=8 << 20, transcendentals=0),
    )(*ins)


def attend_jobs(jobs, n, kid_ref, kv_ref, key_lane):
    scale = HEAD**-0.5 * 1.4426950408889634
    scores, tops, outs = [], [], []
    for q, qid, first in jobs:
        tiles, top = [], None
        for t in range(n):
            at = pl.multiple_of(first + t * TILE, 128)
            keys = kv_ref[pl.ds(at, TILE), key_lane : key_lane + 128]
            s = lax.dot_general(q, keys, (((1,), (1,)), ((), ())), preferred_element_type=jnp.float32)
            s = jnp.where(qid == kid_ref[:, pl.ds(at, TILE)], s, -1e30)
            tiles.append(s)
            most = jnp.maximum(s[:, :128], s[:, 128:])
            top = most if top is None else jnp.maximum(top, most)
        scores.append(tiles)
        tops.append(jnp.max(top, axis=1, keepdims=True))
    for (q, qid, first), tiles, top in zip(jobs, scores, tops):
        total = acc = None
        for t in range(n):
            at = pl.multiple_of(first + t * TILE, 128)
            p = jnp.exp2((tiles[t] - top) * scale)
            part_sum = p[:, :128] + p[:, 128:]
            out = jnp.dot(p.astype(jnp.bfloat16), kv_ref[pl.ds(at, TILE), :], preferred_element_type=jnp.float32)
            total = part_sum if total is None else total + part_sum
            acc = out if acc is None else acc + out
        outs.append(acc * (1.0 / jnp.sum(total, axis=1, keepdims=True)))
    return outs


def attend_kernel(head, info_ref, qid_ref, kid_ref, q_ref, *refs):
    own_refs, (other_ref, out_ref, kv_ref) = refs[:-3], refs[-3:]
    kv_ref[SEQ:, :] = jnp.zeros((TILE, 256), jnp.bfloat16)
    whole, shared = (slice(0, 128), slice(128, 256)) if head == 0 else (slice(128, 256), slice(0, 128))
    for z in range(NZ):
        at = pl.ds(pl.multiple_of(info_ref[z] * FR, FR), FR)
        if head == 0:
            kv_ref[at, :] = own_refs[0][z * FR : (z + 1) * FR, :]
        else:
            kv_ref[at, :128] = own_refs[0][z * FR : (z + 1) * FR, 128:]
            kv_ref[at, 128:] = own_refs[1][z * FR : (z + 1) * FR, :]
        place = info_ref[8 + z] * FR
        kv_ref[pl.ds(pl.multiple_of(place, FR), FR), whole] = other_ref[z, :FR, :]
        packed = other_ref[z, FR:, :]
        kv_ref[pl.ds(pl.multiple_of(place, 96), 96), shared] = packed
        turned = pltpu.roll(packed.astype(jnp.float32), 64, 1).astype(jnp.bfloat16)
        kv_ref[pl.ds(pl.multiple_of(place + 96, 96), 96), shared] = turned

    def pair(g, _):
        slots = [info_ref[32 + 2 * g + i] for i in range(2)]
        count = info_ref[24 + slots[1]]
        jobs = []
        for s in slots:
            rows = pl.ds(pl.multiple_of(s * FR, FR), FR)
            first = jnp.minimum(info_ref[16 + s], PAD - count * TILE)
            jobs.append((q_ref[rows, head * 128 : head * 128 + 128], qid_ref[rows, :], first))

        def attend_pair(n):
            outs = attend_jobs(jobs, n, kid_ref, kv_ref, head * 128)
            lane = lax.broadcasted_iota(jnp.int32, (FR, 128), 1)
            spare = (lane[:48] >= 64) & (lane[:48] < 96) if head == 0 else (lane[:48] >= 32) & (lane[:48] < 64)
            for s, acc in zip(slots, outs):
                m = jnp.where(lane < (64 if head == 0 else 32), acc[:, 128:], acc[:, :128])
                for i, by in enumerate((96, 64, 32)):
                    moved = jnp.where(spare, pltpu.roll(m[144:], by, 1), m[i * 48 : (i + 1) * 48])
                    out_ref[s, i * 48 : (i + 1) * 48, :] = moved.astype(jnp.bfloat16)

        for n in range(1, MAX_TILES + 1):
            pl.when(count == n)(functools.partial(attend_pair, n))
        return 0

    lax.fori_loop(0, NZ // 2, pair, 0)


def attend(head, *args):
    return pl.pallas_call(
        functools.partial(attend_kernel, head),
        in_specs=[SMEM] + [VMEM] * (len(args) - 1),
        out_specs=VMEM,
        out_shape=jax.ShapeDtypeStruct((NZ, 144, 128), jnp.bfloat16),
        scratch_shapes=[pltpu.VMEM((PAD, 256), jnp.bfloat16)],
        compiler_params=pltpu.CompilerParams(vmem_limit_bytes=36 << 20),
        cost_estimate=pl.CostEstimate(flops=4 << 30, bytes_accessed=4 << 20, transcendentals=2 << 20),
    )(*args)


def unpack_kernel(first_ref, second_ref, out_ref):
    lane = lax.broadcasted_iota(jnp.int32, (FR, 128), 1)
    for z in range(0, NZ, 2):
        heads = []
        for i in (z, z + 1):
            for head, ref in enumerate((first_ref, second_ref)):
                m = ref[i].astype(jnp.float32)
                tail = [pltpu.roll(m[j * 48 : (j + 1) * 48], by, 1) for j, by in enumerate((32, 64, 96))]
                if head == 0:
                    parts = jnp.where(lane[:48] >= 96, tail[0], jnp.where(lane[:48] < 32, tail[1], tail[2]))
                else:
                    parts = jnp.where(lane[:48] < 32, tail[2], jnp.where(lane[:48] < 96, tail[0], tail[1]))
                m = jnp.concatenate([m, parts], axis=0)
                heads.append(pltpu.roll(m, 32 if head == 0 else 64, 1))
        a, b, c, d = heads
        tiles = (
            jnp.where(lane < 96, a, pltpu.roll(b, 96, 1)),
            jnp.where(lane < 64, pltpu.roll(b, 96, 1), pltpu.roll(c, 64, 1)),
            jnp.where(lane < 32, pltpu.roll(c, 64, 1), pltpu.roll(d, 32, 1)),
        )
        for i, tile in enumerate(tiles):
            out_ref[:, z * 192 + i * 128 : z * 192 + (i + 1) * 128] = tile.astype(jnp.bfloat16)


def unpack(first, second):
    return pl.pallas_call(
        unpack_kernel,
        in_specs=[VMEM] * 2,
        out_specs=VMEM,
        out_shape=jax.ShapeDtypeStruct((FR, D), jnp.bfloat16),
        compiler_params=pltpu.CompilerParams(vmem_limit_bytes=8 << 20),
    )(first, second)


def plan(ids, order, xh):
    blocks = ids.reshape(16, FR)
    places = order.reshape(NZ, 2)
    own = jnp.where(xh == 0, places[:, 0], places[:, 1])
    other = jnp.where(xh == 0, places[:, 1], places[:, 0])
    qid = jnp.take(blocks, own, axis=0)
    first = jnp.sum(ids[None, :] < qid[:, :1], axis=1, dtype=jnp.int32)
    last = jnp.sum(ids[None, :] <= qid[:, FR - 1 :], axis=1, dtype=jnp.int32)
    first = first // 128 * 128
    count = (last - first + TILE - 1) // TILE
    i = jnp.arange(NZ, dtype=jnp.int32)
    ahead = (count[None, :] < count[:, None]) | ((count[None, :] == count[:, None]) & (i[None, :] < i[:, None]))
    rank = jnp.sum(ahead, axis=1, dtype=jnp.int32)
    ranked = jnp.sum(jnp.where(rank[:, None] == i[None, :], i[:, None], 0), axis=0, dtype=jnp.int32)
    info = jnp.concatenate([own, other, first, count, ranked])
    kid = jnp.concatenate([ids, jnp.full((TILE,), -1, jnp.int32)])[None]
    return info, qid.reshape(ROWS, 1), kid


def body(frames, seg_ids, assign, w_qkv):
    x = lax.all_gather(frames, "z", axis=0, tiled=True)
    w = gather_weights(w_qkv)
    info, qid, kid = plan(seg_ids[0], assign[0], lax.axis_index("xh"))
    x, w, info, qid, kid = lax.optimization_barrier((x, w, info, qid, kid))
    kv, wire0 = project_call(project_first, [256], (x, w), [256])
    other0 = swap(wire0, "xh")
    last, q, wire1 = project_call(project_second, [128, 256], (x, w, kv), [640, 256])
    other1 = swap(wire1, "xh")
    packed0 = attend(0, info, qid, kid, q, kv, other0)
    home0 = lax.all_to_all(packed0, "z", 0, 0, tiled=True)
    packed1 = attend(1, info, qid, kid, q, kv, last, other1)
    home1 = lax.all_to_all(packed1, "z", 0, 0, tiled=True)
    return unpack(home0, home1)


def solution(mesh):
    fine = Mesh(mesh.devices.reshape(SIZES), AXES)
    dp, ctx = AXES[:3], AXES[3:]
    return jax.shard_map(
        body,
        mesh=fine,
        in_specs=(P(AXES, None), P(dp, None), P(dp, None), P(None, dp, ctx)),
        out_specs=P(AXES, None),
        check_vma=False,
    )
```

```python
import functools

import jax
import jax.numpy as jnp
from jax import lax
from jax.experimental import pallas as pl
from jax.experimental.pallas import tpu as pltpu
from jax.sharding import Mesh
from jax.sharding import PartitionSpec as P

HEAD = 96
FR = 192
D = 1536
NZ = 8
ROWS = NZ * FR
SEQ = 3072
TILE = 256
MAX_TILES = 8
PAD = SEQ + TILE
AXES = ("y", "xl", "core", "z", "xh")
SIZES = (8, 2, 2, 8, 2)
VMEM = pl.BlockSpec(memory_space=pltpu.VMEM)
SMEM = pl.BlockSpec(memory_space=pltpu.SMEM)
HBM = pl.BlockSpec(memory_space=pltpu.HBM)


def swap(x, axis):
    return lax.ppermute(x, axis, [(0, 1), (1, 0)])


def both(own, other, index, axis):
    first = jnp.where(index == 0, own, other)
    second = jnp.where(index == 0, other, own)
    return jnp.stack([first, second], axis=axis)


def gather_weights(w):
    flat = jnp.transpose(w, (1, 0, 2)).reshape(w.shape[1], 3 * HEAD)
    heads = both(flat, swap(flat, "xh"), lax.axis_index("xh"), 0)
    q, k, v = (heads[:, :, t * HEAD : (t + 1) * HEAD] for t in range(3))
    shard = jnp.concatenate([k[0], v[0], v[1], k[1], q[0], jnp.zeros_like(q[0, :, :64]), q[1]], axis=1)
    rows = lax.all_to_all(jnp.broadcast_to(shard[None], (8,) + shard.shape), "y", 0, 0, tiled=True)
    rows = both(rows, swap(rows, "xl"), lax.axis_index("xl"), 1)
    rows = both(rows, swap(rows, "core"), lax.axis_index("core"), 2)
    return rows.reshape(D, shard.shape[1])


def project_kernel(x_ref, w_ref, most_ref, last_ref, q_ref):
    y = jnp.dot(x_ref[...], w_ref[...], preferred_element_type=jnp.float32).astype(jnp.bfloat16)
    most_ref[...] = y[:, :256]
    last_ref[...] = y[:, 256:384]
    q_ref[...] = y[:, 384:]


def project(x, w, step=ROWS // 2):
    row = lambda width: pl.BlockSpec((step, width), lambda i: (i, 0))
    widths = (256, 128, 256)
    return pl.pallas_call(
        project_kernel,
        grid=(ROWS // step,),
        in_specs=[row(D), VMEM],
        out_specs=[row(width) for width in widths],
        out_shape=[jax.ShapeDtypeStruct((ROWS, width), jnp.bfloat16) for width in widths],
        compiler_params=pltpu.CompilerParams(vmem_limit_bytes=56 << 20),
        cost_estimate=pl.CostEstimate(flops=2 * ROWS * D * 640, bytes_accessed=10 << 20, transcendentals=0),
    )(x, w)


def attend_jobs(jobs, n, kid_ref, kv_ref, key_lane):
    scale = HEAD**-0.5 * 1.4426950408889634
    scores, tops, outs = [], [], []
    for q, qid, first in jobs:
        tiles, top = [], None
        for t in range(n):
            at = pl.multiple_of(first + t * TILE, 128)
            keys = kv_ref[pl.ds(at, TILE), key_lane : key_lane + 128]
            s = lax.dot_general(q, keys, (((1,), (1,)), ((), ())), preferred_element_type=jnp.float32)
            s = jnp.where(qid == kid_ref[:, pl.ds(at, TILE)], s, -1e30)
            tiles.append(s)
            most = jnp.maximum(s[:, :128], s[:, 128:])
            top = most if top is None else jnp.maximum(top, most)
        scores.append(tiles)
        tops.append(jnp.max(top, axis=1, keepdims=True))
    for (q, qid, first), tiles, top in zip(jobs, scores, tops):
        total = acc = None
        for t in range(n):
            at = pl.multiple_of(first + t * TILE, 128)
            p = jnp.exp2((tiles[t] - top) * scale)
            part_sum = p[:, :128] + p[:, 128:]
            out = jnp.dot(p.astype(jnp.bfloat16), kv_ref[pl.ds(at, TILE), :], preferred_element_type=jnp.float32)
            total = part_sum if total is None else total + part_sum
            acc = out if acc is None else acc + out
        outs.append(acc * (1.0 / jnp.sum(total, axis=1, keepdims=True)))
    return outs


def attend_kernel(head, group, info_ref, qid_ref, kid_ref, q_hbm, *refs):
    *parts, out_ref, kv_ref, q_ref, sems = refs
    copies = [pltpu.make_async_copy(q_hbm.at[:, head * 128 : head * 128 + 128], q_ref, sems.at[0])]
    for z in range(NZ):
        rows = pl.ds(z * FR, FR)
        for side in range(2):
            at = pl.ds(pl.multiple_of(info_ref[side * NZ + z] * FR, FR), FR)
            sem = 1 + 4 * z + 2 * side
            if head == 0:
                copies.append(pltpu.make_async_copy(parts[side].at[rows, :], kv_ref.at[at, :], sems.at[sem]))
            else:
                most, last = parts[side], parts[2 + side]
                copies.append(pltpu.make_async_copy(most.at[rows, 128:], kv_ref.at[at, :128], sems.at[sem]))
                copies.append(pltpu.make_async_copy(last.at[rows, :], kv_ref.at[at, 128:], sems.at[sem + 1]))
    for copy in copies:
        copy.start()
    kv_ref[SEQ:, :] = jnp.zeros((TILE, 256), jnp.bfloat16)
    for copy in copies:
        copy.wait()

    def some(g, _):
        slots = [info_ref[32 + group * g + i] for i in range(group)]
        count = info_ref[24 + slots[-1]]
        jobs = []
        for s in slots:
            rows = pl.ds(pl.multiple_of(s * FR, FR), FR)
            first = jnp.minimum(info_ref[16 + s], PAD - count * TILE)
            jobs.append((q_ref[rows, :], qid_ref[rows, :], first))

        def attend_some(n):
            outs = attend_jobs(jobs, n, kid_ref, kv_ref, head * 128)
            lane = lax.broadcasted_iota(jnp.int32, (FR, 128), 1)
            spare = (lane[:48] >= 64) & (lane[:48] < 96) if head == 0 else (lane[:48] >= 32) & (lane[:48] < 64)
            for s, acc in zip(slots, outs):
                m = jnp.where(lane < (64 if head == 0 else 32), acc[:, 128:], acc[:, :128])
                for i, by in enumerate((96, 64, 32)):
                    moved = jnp.where(spare, pltpu.roll(m[144:], by, 1), m[i * 48 : (i + 1) * 48])
                    out_ref[s, i * 48 : (i + 1) * 48, :] = moved.astype(jnp.bfloat16)

        for n in range(1, MAX_TILES + 1):
            pl.when(count == n)(functools.partial(attend_some, n))
        return 0

    lax.fori_loop(0, NZ // group, some, 0)


def attend(head, info, qid, kid, q, *parts, group=2):
    return pl.pallas_call(
        functools.partial(attend_kernel, head, group),
        in_specs=[SMEM, VMEM, VMEM] + [HBM] * (1 + len(parts)),
        out_specs=VMEM,
        out_shape=jax.ShapeDtypeStruct((NZ, 144, 128), jnp.bfloat16),
        scratch_shapes=[
            pltpu.VMEM((PAD, 256), jnp.bfloat16),
            pltpu.VMEM((ROWS, 128), jnp.bfloat16),
            pltpu.SemaphoreType.DMA((1 + 4 * NZ,)),
        ],
        compiler_params=pltpu.CompilerParams(vmem_limit_bytes=36 << 20),
        cost_estimate=pl.CostEstimate(flops=4 << 30, bytes_accessed=4 << 20, transcendentals=2 << 20),
    )(info, qid, kid, q, *parts)


def unpack_kernel(first_ref, second_ref, out_ref):
    lane = lax.broadcasted_iota(jnp.int32, (FR, 128), 1)
    for z in range(0, NZ, 2):
        heads = []
        for i in (z, z + 1):
            for head, ref in enumerate((first_ref, second_ref)):
                m = ref[i].astype(jnp.float32)
                tail = [pltpu.roll(m[j * 48 : (j + 1) * 48], by, 1) for j, by in enumerate((32, 64, 96))]
                if head == 0:
                    parts = jnp.where(lane[:48] >= 96, tail[0], jnp.where(lane[:48] < 32, tail[1], tail[2]))
                else:
                    parts = jnp.where(lane[:48] < 32, tail[2], jnp.where(lane[:48] < 96, tail[0], tail[1]))
                m = jnp.concatenate([m, parts], axis=0)
                heads.append(pltpu.roll(m, 32 if head == 0 else 64, 1))
        a, b, c, d = heads
        tiles = (
            jnp.where(lane < 96, a, pltpu.roll(b, 96, 1)),
            jnp.where(lane < 64, pltpu.roll(b, 96, 1), pltpu.roll(c, 64, 1)),
            jnp.where(lane < 32, pltpu.roll(c, 64, 1), pltpu.roll(d, 32, 1)),
        )
        for i, tile in enumerate(tiles):
            out_ref[:, z * 192 + i * 128 : z * 192 + (i + 1) * 128] = tile.astype(jnp.bfloat16)


def unpack(first, second):
    return pl.pallas_call(
        unpack_kernel,
        in_specs=[VMEM] * 2,
        out_specs=VMEM,
        out_shape=jax.ShapeDtypeStruct((FR, D), jnp.bfloat16),
        compiler_params=pltpu.CompilerParams(vmem_limit_bytes=8 << 20),
    )(first, second)


def plan(ids, order, xh):
    blocks = ids.reshape(16, FR)
    places = order.reshape(NZ, 2)
    own = jnp.where(xh == 0, places[:, 0], places[:, 1])
    other = jnp.where(xh == 0, places[:, 1], places[:, 0])
    qid = jnp.take(blocks, own, axis=0)
    first = jnp.sum(ids[None, :] < qid[:, :1], axis=1, dtype=jnp.int32)
    last = jnp.sum(ids[None, :] <= qid[:, FR - 1 :], axis=1, dtype=jnp.int32)
    first = first // 128 * 128
    count = (last - first + TILE - 1) // TILE
    i = jnp.arange(NZ, dtype=jnp.int32)
    ahead = (count[None, :] < count[:, None]) | ((count[None, :] == count[:, None]) & (i[None, :] < i[:, None]))
    rank = jnp.sum(ahead, axis=1, dtype=jnp.int32)
    ranked = jnp.sum(jnp.where(rank[:, None] == i[None, :], i[:, None], 0), axis=0, dtype=jnp.int32)
    info = jnp.concatenate([own, other, first, count, ranked])
    kid = jnp.concatenate([ids, jnp.full((TILE,), -1, jnp.int32)])[None]
    return info, qid.reshape(ROWS, 1), kid


def body(frames, seg_ids, assign, w_qkv):
    x = lax.all_gather(frames, "z", axis=0, tiled=True)
    w = gather_weights(w_qkv)
    info, qid, kid = plan(seg_ids[0], assign[0], lax.axis_index("xh"))
    x, w, info, qid, kid = lax.optimization_barrier((x, w, info, qid, kid))
    most, last, q = project(x, w)
    other_most, other_last = swap(most, "xh"), swap(last, "xh")
    home0 = lax.all_to_all(attend(0, info, qid, kid, q, most, other_most), "z", 0, 0, tiled=True)
    packed1 = attend(1, info, qid, kid, q, most, other_most, last, other_last)
    home1 = lax.all_to_all(packed1, "z", 0, 0, tiled=True)
    return unpack(home0, home1)


def solution(mesh):
    fine = Mesh(mesh.devices.reshape(SIZES), AXES)
    dp, ctx = AXES[:3], AXES[3:]
    return jax.shard_map(
        body,
        mesh=fine,
        in_specs=(P(AXES, None), P(dp, None), P(dp, None), P(None, dp, ctx)),
        out_specs=P(AXES, None),
        check_vma=False,
    )
```

```python
import functools

import jax
import jax.numpy as jnp
from jax import lax
from jax.experimental import pallas as pl
from jax.experimental.pallas import tpu as pltpu
from jax.sharding import Mesh
from jax.sharding import PartitionSpec as P

HEAD = 96
FR = 192
D = 1536
NZ = 8
ROWS = NZ * FR
SEQ = 3072
TILE = 256
MAX_TILES = 8
PAD = SEQ + TILE
AXES = ("y", "xl", "core", "z", "xh")
SIZES = (8, 2, 2, 8, 2)
VMEM = pl.BlockSpec(memory_space=pltpu.VMEM)
SMEM = pl.BlockSpec(memory_space=pltpu.SMEM)


def swap(x, axis):
    return lax.ppermute(x, axis, [(0, 1), (1, 0)])


def both(own, other, index, axis):
    first = jnp.where(index == 0, own, other)
    second = jnp.where(index == 0, other, own)
    return jnp.stack([first, second], axis=axis)


def gather_weights(w):
    flat = jnp.transpose(w, (1, 0, 2)).reshape(w.shape[1], 3 * HEAD)
    heads = both(flat, swap(flat, "xh"), lax.axis_index("xh"), 0)
    q, k, v = (heads[:, :, t * HEAD : (t + 1) * HEAD] for t in range(3))
    shard = jnp.concatenate([k[0], v[0], v[1], k[1], q[0], jnp.zeros_like(q[0, :, :64]), q[1]], axis=1)
    rows = lax.all_to_all(jnp.broadcast_to(shard[None], (8,) + shard.shape), "y", 0, 0, tiled=True)
    rows = both(rows, swap(rows, "xl"), lax.axis_index("xl"), 1)
    rows = both(rows, swap(rows, "core"), lax.axis_index("core"), 2)
    return rows.reshape(D, shard.shape[1])


def project_kernel(x_ref, w_ref, most_ref, last_ref, q_ref):
    y = jnp.dot(x_ref[...], w_ref[...], preferred_element_type=jnp.float32).astype(jnp.bfloat16)
    most_ref[...] = y[:, :256]
    last_ref[...] = y[:, 256:384]
    q_ref[...] = y[:, 384:]


def project(x, w, step=ROWS // 2):
    row = lambda width: pl.BlockSpec((step, width), lambda i: (i, 0))
    widths = (256, 128, 256)
    return pl.pallas_call(
        project_kernel,
        grid=(ROWS // step,),
        in_specs=[row(D), VMEM],
        out_specs=[row(width) for width in widths],
        out_shape=[jax.ShapeDtypeStruct((ROWS, width), jnp.bfloat16) for width in widths],
        compiler_params=pltpu.CompilerParams(vmem_limit_bytes=24 << 20),
        cost_estimate=pl.CostEstimate(flops=2 * ROWS * D * 640, bytes_accessed=10 << 20, transcendentals=0),
    )(x, w)


def attend_jobs(jobs, n, kid_ref, kv_ref, key_lane):
    scale = HEAD**-0.5 * 1.4426950408889634
    scores, tops, outs = [], [], []
    for q, qid, first in jobs:
        tiles, top = [], None
        for t in range(n):
            at = pl.multiple_of(first + t * TILE, 128)
            keys = kv_ref[pl.ds(at, TILE), key_lane : key_lane + 128]
            s = lax.dot_general(q, keys, (((1,), (1,)), ((), ())), preferred_element_type=jnp.float32)
            s = jnp.where(qid == kid_ref[:, pl.ds(at, TILE)], s, -1e30)
            tiles.append(s)
            most = jnp.maximum(s[:, :128], s[:, 128:])
            top = most if top is None else jnp.maximum(top, most)
        scores.append(tiles)
        tops.append(jnp.max(top, axis=1, keepdims=True))
    for (q, qid, first), tiles, top in zip(jobs, scores, tops):
        total = acc = None
        for t in range(n):
            at = pl.multiple_of(first + t * TILE, 128)
            p = jnp.exp2((tiles[t] - top) * scale)
            part_sum = p[:, :128] + p[:, 128:]
            out = jnp.dot(p.astype(jnp.bfloat16), kv_ref[pl.ds(at, TILE), :], preferred_element_type=jnp.float32)
            total = part_sum if total is None else total + part_sum
            acc = out if acc is None else acc + out
        outs.append(acc * (1.0 / jnp.sum(total, axis=1, keepdims=True)))
    return outs


def attend_kernel(head, group, info_ref, qid_ref, kid_ref, q_ref, *refs):
    *parts, out_ref, kv_ref = refs
    kv_ref[SEQ:, :] = jnp.zeros((TILE, 256), jnp.bfloat16)
    if head == 1:
        out_ref[:, :144, :] = parts[4][...]
    for z in range(NZ):
        rows = slice(z * FR, (z + 1) * FR)
        for side in range(2):
            at = pl.ds(pl.multiple_of(info_ref[side * NZ + z] * FR, FR), FR)
            if head == 0:
                kv_ref[at, :] = parts[side][rows, :]
            else:
                kv_ref[at, :128] = parts[side][rows, 128:]
                kv_ref[at, 128:] = parts[2 + side][rows, :]

    def some(g, _):
        slots = [info_ref[32 + group * g + i] for i in range(group)]
        count = info_ref[24 + slots[-1]]
        jobs = []
        for s in slots:
            rows = pl.ds(pl.multiple_of(s * FR, FR), FR)
            first = jnp.minimum(info_ref[16 + s], PAD - count * TILE)
            jobs.append((q_ref[rows, head * 128 : head * 128 + 128], qid_ref[rows, :], first))

        def attend_some(n):
            outs = attend_jobs(jobs, n, kid_ref, kv_ref, head * 128)
            lane = lax.broadcasted_iota(jnp.int32, (FR, 128), 1)
            spare = (lane[:48] >= 64) & (lane[:48] < 96) if head == 0 else (lane[:48] >= 32) & (lane[:48] < 64)
            for s, acc in zip(slots, outs):
                m = jnp.where(lane < (64 if head == 0 else 32), acc[:, 128:], acc[:, :128])
                for i, by in enumerate((96, 64, 32)):
                    moved = jnp.where(spare, pltpu.roll(m[144:], by, 1), m[i * 48 : (i + 1) * 48])
                    out_ref[s, head * 144 + i * 48 : head * 144 + (i + 1) * 48, :] = moved.astype(jnp.bfloat16)

        for n in range(1, MAX_TILES + 1):
            pl.when(count == n)(functools.partial(attend_some, n))
        return 0

    lax.fori_loop(0, NZ // group, some, 0)


def attend(head, info, qid, kid, q, *parts, group=2):
    return pl.pallas_call(
        functools.partial(attend_kernel, head, group),
        in_specs=[SMEM, VMEM, VMEM] + [VMEM] * (1 + len(parts)),
        out_specs=VMEM,
        out_shape=jax.ShapeDtypeStruct((NZ, 144 * (1 + head), 128), jnp.bfloat16),
        scratch_shapes=[pltpu.VMEM((PAD, 256), jnp.bfloat16)],
        compiler_params=pltpu.CompilerParams(vmem_limit_bytes=28 << 20),
        cost_estimate=pl.CostEstimate(flops=4 << 30, bytes_accessed=4 << 20, transcendentals=2 << 20),
    )(info, qid, kid, q, *parts)


def unpack_kernel(in_ref, out_ref):
    lane = lax.broadcasted_iota(jnp.int32, (FR, 128), 1)
    for z in range(0, NZ, 2):
        heads = []
        for i in (z, z + 1):
            for head in range(2):
                m = in_ref[i, head * 144 : (head + 1) * 144, :].astype(jnp.float32)
                tail = [pltpu.roll(m[j * 48 : (j + 1) * 48], by, 1) for j, by in enumerate((32, 64, 96))]
                if head == 0:
                    parts = jnp.where(lane[:48] >= 96, tail[0], jnp.where(lane[:48] < 32, tail[1], tail[2]))
                else:
                    parts = jnp.where(lane[:48] < 32, tail[2], jnp.where(lane[:48] < 96, tail[0], tail[1]))
                m = jnp.concatenate([m, parts], axis=0)
                heads.append(pltpu.roll(m, 32 if head == 0 else 64, 1))
        a, b, c, d = heads
        tiles = (
            jnp.where(lane < 96, a, pltpu.roll(b, 96, 1)),
            jnp.where(lane < 64, pltpu.roll(b, 96, 1), pltpu.roll(c, 64, 1)),
            jnp.where(lane < 32, pltpu.roll(c, 64, 1), pltpu.roll(d, 32, 1)),
        )
        for i, tile in enumerate(tiles):
            out_ref[:, z * 192 + i * 128 : z * 192 + (i + 1) * 128] = tile.astype(jnp.bfloat16)


def unpack(packed):
    return pl.pallas_call(
        unpack_kernel,
        in_specs=[VMEM],
        out_specs=VMEM,
        out_shape=jax.ShapeDtypeStruct((FR, D), jnp.bfloat16),
        compiler_params=pltpu.CompilerParams(vmem_limit_bytes=8 << 20),
    )(packed)


def plan(ids, order, xh):
    blocks = ids.reshape(16, FR)
    places = order.reshape(NZ, 2)
    own = jnp.where(xh == 0, places[:, 0], places[:, 1])
    other = jnp.where(xh == 0, places[:, 1], places[:, 0])
    qid = jnp.take(blocks, own, axis=0)
    first = jnp.sum(ids[None, :] < qid[:, :1], axis=1, dtype=jnp.int32)
    last = jnp.sum(ids[None, :] <= qid[:, FR - 1 :], axis=1, dtype=jnp.int32)
    first = first // 128 * 128
    count = (last - first + TILE - 1) // TILE
    i = jnp.arange(NZ, dtype=jnp.int32)
    ahead = (count[None, :] < count[:, None]) | ((count[None, :] == count[:, None]) & (i[None, :] < i[:, None]))
    rank = jnp.sum(ahead, axis=1, dtype=jnp.int32)
    ranked = jnp.sum(jnp.where(rank[:, None] == i[None, :], i[:, None], 0), axis=0, dtype=jnp.int32)
    info = jnp.concatenate([own, other, first, count, ranked])
    kid = jnp.concatenate([ids, jnp.full((TILE,), -1, jnp.int32)])[None]
    return info, qid.reshape(ROWS, 1), kid


def body(frames, seg_ids, assign, w_qkv):
    x = lax.all_gather(frames, "z", axis=0, tiled=True)
    w = gather_weights(w_qkv)
    info, qid, kid = plan(seg_ids[0], assign[0], lax.axis_index("xh"))
    x, w, info, qid, kid = lax.optimization_barrier((x, w, info, qid, kid))
    most, last, q = project(x, w)
    other_most, other_last = swap(most, "xh"), swap(last, "xh")
    packed = attend(0, info, qid, kid, q, most, other_most)
    packed = attend(1, info, qid, kid, q, most, other_most, last, other_last, packed)
    return unpack(lax.all_to_all(packed, "z", 0, 0, tiled=True))


def solution(mesh):
    fine = Mesh(mesh.devices.reshape(SIZES), AXES)
    dp, ctx = AXES[:3], AXES[3:]
    return jax.shard_map(
        body,
        mesh=fine,
        in_specs=(P(AXES, None), P(dp, None), P(dp, None), P(None, dp, ctx)),
        out_specs=P(AXES, None),
        check_vma=False,
    )
```

```python
import functools

import jax
import jax.numpy as jnp
from jax import lax
from jax.experimental import pallas as pl
from jax.experimental.pallas import tpu as pltpu
from jax.sharding import Mesh
from jax.sharding import PartitionSpec as P

HEAD = 96
FR = 192
D = 1536
NZ = 8
ROWS = NZ * FR
SEQ = 3072
TILE = 256
MAX_TILES = 8
PAD = SEQ + TILE
AXES = ("y", "xl", "core", "z", "xh")
SIZES = (8, 2, 2, 8, 2)
VMEM = pl.BlockSpec(memory_space=pltpu.VMEM)
SMEM = pl.BlockSpec(memory_space=pltpu.SMEM)


def swap(x, axis):
    return lax.ppermute(x, axis, [(0, 1), (1, 0)])


def both(own, other, index, axis):
    first = jnp.where(index == 0, own, other)
    second = jnp.where(index == 0, other, own)
    return jnp.stack([first, second], axis=axis)


def gather_weights(w, frames):
    flat = jnp.transpose(w, (1, 0, 2)).reshape(w.shape[1], 3 * HEAD)
    heads = both(flat, swap(flat, "xh"), lax.axis_index("xh"), 0)
    q, k, v = (heads[:, :, t * HEAD : (t + 1) * HEAD] for t in range(3))
    shard = jnp.concatenate([k[0], v[0], v[1], k[1], q[0], jnp.zeros_like(q[0, :, :64]), q[1]], axis=1)
    frames, shard = lax.optimization_barrier((frames, shard))
    partner = swap(frames, "xh")
    rows = lax.all_to_all(jnp.broadcast_to(shard[None], (8,) + shard.shape), "y", 0, 0, tiled=True)
    rows, partner = lax.optimization_barrier((rows, partner))
    rows = both(rows, swap(rows, "xl"), lax.axis_index("xl"), 1)
    rows = both(rows, swap(rows, "core"), lax.axis_index("core"), 2)
    return rows.reshape(D, shard.shape[1]), partner


def project_rows(x, w_ref, rows, most_ref, last_ref):
    y = jnp.dot(x, w_ref[:, :384], preferred_element_type=jnp.float32).astype(jnp.bfloat16)
    most_ref[rows, :] = y[:, :256]
    last_ref[rows, :] = y[:, 256:]


def project_near_kernel(own_ref, other_ref, w_ref, *outs):
    x = jnp.concatenate([own_ref[...], other_ref[...]], axis=0)
    project_rows(x, w_ref, slice(0, 2 * FR), *outs)


def project_far_kernel(z_ref, x_ref, w_ref, most_ref, last_ref):
    starts = [pl.multiple_of(lax.rem(z_ref[0] + 1 + i, NZ) * FR, FR) for i in range(7)]
    x = jnp.concatenate([x_ref[pl.ds(start, FR), :] for start in starts], axis=0)
    project_rows(x, w_ref, slice(0, 7 * FR), most_ref, last_ref)


def project_queries_kernel(x_ref, w_ref, q_ref):
    q_ref[...] = jnp.dot(x_ref[...], w_ref[:, 384:], preferred_element_type=jnp.float32).astype(jnp.bfloat16)


def project(kernel, specs, args, rows):
    return pl.pallas_call(
        kernel,
        in_specs=specs,
        out_specs=[VMEM] * 2,
        out_shape=[jax.ShapeDtypeStruct((rows, width), jnp.bfloat16) for width in (256, 128)],
        compiler_params=pltpu.CompilerParams(vmem_limit_bytes=24 << 20),
        cost_estimate=pl.CostEstimate(flops=2 * rows * D * 384, bytes_accessed=rows * D * 4, transcendentals=0),
    )(*args)


def project_near(own, other, w):
    return project(project_near_kernel, [VMEM] * 3, (own, other, w), 2 * FR)


def project_far(z, x, w):
    return project(project_far_kernel, [SMEM, VMEM, VMEM], (z[None], x, w), 7 * FR)


def project_queries(x, w):
    return pl.pallas_call(
        project_queries_kernel,
        in_specs=[VMEM, VMEM],
        out_specs=VMEM,
        out_shape=jax.ShapeDtypeStruct((ROWS, 256), jnp.bfloat16),
        compiler_params=pltpu.CompilerParams(vmem_limit_bytes=24 << 20),
        cost_estimate=pl.CostEstimate(flops=2 * ROWS * D * 256, bytes_accessed=ROWS * D * 3, transcendentals=0),
    )(x, w)


def attend_jobs(jobs, n, kid_ref, kv_ref, key_lane):
    scale = HEAD**-0.5 * 1.4426950408889634
    scores, tops, outs = [], [], []
    for q, qid, first in jobs:
        tiles, top = [], None
        for t in range(n):
            at = pl.multiple_of(first + t * TILE, 128)
            keys = kv_ref[pl.ds(at, TILE), key_lane : key_lane + 128]
            s = lax.dot_general(q, keys, (((1,), (1,)), ((), ())), preferred_element_type=jnp.float32)
            s = jnp.where(qid == kid_ref[:, pl.ds(at, TILE)], s, -1e30)
            tiles.append(s)
            most = jnp.maximum(s[:, :128], s[:, 128:])
            top = most if top is None else jnp.maximum(top, most)
        scores.append(tiles)
        tops.append(jnp.max(top, axis=1, keepdims=True))
    for (q, qid, first), tiles, top in zip(jobs, scores, tops):
        total = acc = None
        for t in range(n):
            at = pl.multiple_of(first + t * TILE, 128)
            p = jnp.exp2((tiles[t] - top) * scale)
            part_sum = p[:, :128] + p[:, 128:]
            out = jnp.dot(p.astype(jnp.bfloat16), kv_ref[pl.ds(at, TILE), :], preferred_element_type=jnp.float32)
            total = part_sum if total is None else total + part_sum
            acc = out if acc is None else acc + out
        outs.append(acc * (1.0 / jnp.sum(total, axis=1, keepdims=True)))
    return outs


def attend_kernel(head, group, info_ref, qid_ref, kid_ref, q_ref, *refs):
    *parts, out_ref, kv_ref = refs
    kv_ref[SEQ:, :] = jnp.zeros((TILE, 256), jnp.bfloat16)
    for s in range(NZ):
        for side in range(2):
            at = pl.ds(pl.multiple_of(info_ref[side * NZ + s] * FR, FR), FR)
            which, i = (side, s) if s < 7 else (2, side)
            rows = slice(i * FR, (i + 1) * FR)
            if head == 0:
                kv_ref[at, :] = parts[which][rows, :]
            else:
                kv_ref[at, :128] = parts[which][rows, 128:]
                kv_ref[at, 128:] = parts[3 + which][rows, :]

    def some(g, _):
        slots = [info_ref[32 + group * g + i] for i in range(group)]
        count = info_ref[24 + slots[-1]]
        jobs = []
        for s in slots:
            rows = pl.ds(pl.multiple_of(s * FR, FR), FR)
            query_rows = pl.ds(pl.multiple_of(info_ref[40 + s] * FR, FR), FR)
            first = jnp.minimum(info_ref[16 + s], PAD - count * TILE)
            jobs.append((q_ref[query_rows, head * 128 : head * 128 + 128], qid_ref[rows, :], first))

        def attend_some(n):
            outs = attend_jobs(jobs, n, kid_ref, kv_ref, head * 128)
            lane = lax.broadcasted_iota(jnp.int32, (FR, 128), 1)
            for s, acc in zip(slots, outs):
                z = info_ref[40 + s]
                if head == 0:
                    out_ref[z] = jnp.where(lane < 64, acc[:, 128:], acc[:, :128]).astype(jnp.bfloat16)
                    continue
                spare = (lane >= 64) & (lane < 96)
                first = jnp.where(spare, pltpu.roll(acc[:, 128:], 64, 1), parts[6][z].astype(jnp.float32))
                out_ref[z, :FR, :] = first.astype(jnp.bfloat16)
                upper, lower = acc[: FR // 2, :128], acc[FR // 2 :, :128]
                both_rows = jnp.where(lane[: FR // 2] < 64, pltpu.roll(lower, 64, 1), upper)
                out_ref[z, FR:, :] = both_rows.astype(jnp.bfloat16)

        for n in range(1, MAX_TILES + 1):
            pl.when(count == n)(functools.partial(attend_some, n))
        return 0

    lax.fori_loop(0, NZ // group, some, 0)


def attend(head, info, qid, kid, *parts, group=2):
    return pl.pallas_call(
        functools.partial(attend_kernel, head, group),
        in_specs=[SMEM, VMEM, VMEM] + [VMEM] * len(parts),
        out_specs=VMEM,
        out_shape=jax.ShapeDtypeStruct((NZ, (FR, FR * 3 // 2)[head], 128), jnp.bfloat16),
        scratch_shapes=[pltpu.VMEM((PAD, 256), jnp.bfloat16)],
        compiler_params=pltpu.CompilerParams(vmem_limit_bytes=28 << 20),
        cost_estimate=pl.CostEstimate(flops=4 << 30, bytes_accessed=4 << 20, transcendentals=2 << 20),
    )(info, qid, kid, *parts)


def unpack_kernel(in_ref, out_ref):
    lane = lax.broadcasted_iota(jnp.int32, (FR, 128), 1)
    for z in range(0, NZ, 2):
        tiles = []
        for i in range(2):
            a = in_ref[z + i, :FR, :].astype(jnp.float32)
            b = in_ref[z + i, FR:, :].astype(jnp.float32)
            tiles.append((pltpu.roll(a, 32, 1), pltpu.roll(a, 96, 1)))
            tiles.append([jnp.concatenate([pltpu.roll(b, by, 1), pltpu.roll(b, by + 64, 1)], axis=0) for by in (32, 96)[i : i + 1]])
        (a32, a96), (b32,), (c32, c96), (d96,) = tiles
        out = (
            jnp.where(lane < 96, a32, b32),
            jnp.where(lane < 32, b32, jnp.where(lane < 64, a96, c96)),
            jnp.where(lane < 32, c96, jnp.where(lane < 96, d96, c32)),
        )
        for i, tile in enumerate(out):
            out_ref[:, z * 192 + i * 128 : z * 192 + (i + 1) * 128] = tile.astype(jnp.bfloat16)


def unpack(packed):
    return pl.pallas_call(
        unpack_kernel,
        in_specs=[VMEM],
        out_specs=VMEM,
        out_shape=jax.ShapeDtypeStruct((FR, D), jnp.bfloat16),
        compiler_params=pltpu.CompilerParams(vmem_limit_bytes=8 << 20),
    )(packed)


def plan(ids, order, z, xh):
    blocks = ids.reshape(16, FR)
    zs = (z + 1 + jnp.arange(NZ, dtype=jnp.int32)) % NZ
    places = jnp.take(order.reshape(NZ, 2), zs, axis=0)
    own = jnp.where(xh == 0, places[:, 0], places[:, 1])
    other = jnp.where(xh == 0, places[:, 1], places[:, 0])
    qid = jnp.take(blocks, own, axis=0)
    first = jnp.sum(ids[None, :] < qid[:, :1], axis=1, dtype=jnp.int32)
    last = jnp.sum(ids[None, :] <= qid[:, FR - 1 :], axis=1, dtype=jnp.int32)
    first = first // 128 * 128
    count = (last - first + TILE - 1) // TILE
    i = jnp.arange(NZ, dtype=jnp.int32)
    ahead = (count[None, :] < count[:, None]) | ((count[None, :] == count[:, None]) & (i[None, :] < i[:, None]))
    rank = jnp.sum(ahead, axis=1, dtype=jnp.int32)
    ranked = jnp.sum(jnp.where(rank[:, None] == i[None, :], i[:, None], 0), axis=0, dtype=jnp.int32)
    info = jnp.concatenate([own, other, first, count, ranked, zs])
    kid = jnp.concatenate([ids, jnp.full((TILE,), -1, jnp.int32)])[None]
    return info, qid.reshape(ROWS, 1), kid


def body(frames, seg_ids, assign, w_qkv):
    z, xh = lax.axis_index("z").astype(jnp.int32), lax.axis_index("xh")
    x = lax.all_gather(frames, "z", axis=0, tiled=True)
    w, partner = gather_weights(w_qkv, frames)
    near_most, near_last = project_near(frames, partner, w)
    info, qid, kid = plan(seg_ids[0], assign[0], z, xh)
    x, info, qid, kid, near_last = lax.optimization_barrier((x, info, qid, kid, near_last))
    most, last = project_far(z, x, w)
    other_most, other_last = swap(most, "xh"), swap(last, "xh")
    mosts, lasts = (most, other_most, near_most), (last, other_last, near_last)
    q = project_queries(x, w)
    packed = attend(0, info, qid, kid, q, *mosts)
    packed = attend(1, info, qid, kid, q, *mosts, *lasts, packed)
    return unpack(lax.all_to_all(packed, "z", 0, 0, tiled=True))


def solution(mesh):
    fine = Mesh(mesh.devices.reshape(SIZES), AXES)
    dp, ctx = AXES[:3], AXES[3:]
    return jax.shard_map(
        body,
        mesh=fine,
        in_specs=(P(AXES, None), P(dp, None), P(dp, None), P(None, dp, ctx)),
        out_specs=P(AXES, None),
        check_vma=False,
    )
```

```python
import functools

import jax
import jax.numpy as jnp
from jax import lax
from jax.experimental import pallas as pl
from jax.experimental.pallas import tpu as pltpu
from jax.sharding import Mesh
from jax.sharding import PartitionSpec as P

HEAD = 96
FR = 192
D = 1536
NZ = 8
ROWS = NZ * FR
SEQ = 3072
TILE = 256
MAX_TILES = 8
PAD = SEQ + TILE
AXES = ("y", "xl", "core", "z", "xh")
SIZES = (8, 2, 2, 8, 2)
VMEM = pl.BlockSpec(memory_space=pltpu.VMEM)
SMEM = pl.BlockSpec(memory_space=pltpu.SMEM)


def swap(x, axis):
    return lax.ppermute(x, axis, [(0, 1), (1, 0)])


def both(own, other, index, axis):
    first = jnp.where(index == 0, own, other)
    second = jnp.where(index == 0, other, own)
    return jnp.stack([first, second], axis=axis)


def gather_weights(w, frames):
    flat = jnp.transpose(w, (1, 0, 2)).reshape(w.shape[1], 3 * HEAD)
    heads = both(flat, swap(flat, "xh"), lax.axis_index("xh"), 0)
    q, k, v = (heads[:, :, t * HEAD : (t + 1) * HEAD] for t in range(3))
    shard = jnp.concatenate([k[0], v[0], v[1], k[1], q[0], jnp.zeros_like(q[0, :, :64]), q[1]], axis=1)
    frames, shard = lax.optimization_barrier((frames, shard))
    partner = swap(frames, "xh")
    rows = lax.all_to_all(jnp.broadcast_to(shard[None], (8,) + shard.shape), "y", 0, 0, tiled=True)
    rows, partner = lax.optimization_barrier((rows, partner))
    rows = both(rows, swap(rows, "xl"), lax.axis_index("xl"), 1)
    rows = both(rows, swap(rows, "core"), lax.axis_index("core"), 2)
    return rows.reshape(D, shard.shape[1]), partner


def project_near_kernel(x_ref, w_ref, most_ref, last_ref):
    y = jnp.dot(x_ref[...], w_ref[:, :384], preferred_element_type=jnp.float32).astype(jnp.bfloat16)
    most_ref[...] = y[:, :256]
    last_ref[...] = y[:, 256:]


def project_wires_kernel(z_ref, x_ref, w_ref, first_ref, second_ref):
    starts = [pl.multiple_of(lax.rem(z_ref[0] + 1 + i, NZ) * FR, FR) for i in range(7)]
    x = jnp.concatenate([x_ref[pl.ds(start, FR), :] for start in starts], axis=0)
    y = jnp.dot(x, w_ref[:, :384], preferred_element_type=jnp.float32)
    half = lax.broadcasted_iota(jnp.int32, (FR // 2, 128), 1) < 64
    for b in range(7):
        block = y[b * FR : (b + 1) * FR]
        first_ref[b, :FR, :] = block[:, :128].astype(jnp.bfloat16)
        second_ref[b, :FR, :] = block[:, 256:].astype(jnp.bfloat16)
        upper, turned = block[: FR // 2, 128:256], pltpu.roll(block[FR // 2 :, 128:256], 64, 1)
        first_ref[b, FR:, :] = jnp.where(half, upper, turned).astype(jnp.bfloat16)
        second_ref[b, FR:, :] = jnp.where(half, turned, upper).astype(jnp.bfloat16)


def project_own_kernel(x_ref, w_ref, most_ref, last_ref, q_ref):
    y = jnp.dot(x_ref[...], w_ref[...], preferred_element_type=jnp.float32).astype(jnp.bfloat16)
    most_ref[...] = y[:, :256]
    last_ref[...] = y[:, 256:384]
    q_ref[...] = y[:, 384:]


def project(kernel, rows, columns, shapes, *args):
    return pl.pallas_call(
        kernel,
        in_specs=[SMEM] * (len(args) - 2) + [VMEM] * 2,
        out_specs=[VMEM] * len(shapes),
        out_shape=[jax.ShapeDtypeStruct(shape, jnp.bfloat16) for shape in shapes],
        compiler_params=pltpu.CompilerParams(vmem_limit_bytes=16 << 20),
        cost_estimate=pl.CostEstimate(
            flops=2 * rows * D * columns, bytes_accessed=rows * D * 4, transcendentals=0
        ),
    )(*args)


def project_near(x, w):
    return project(project_near_kernel, FR, 384, [(FR, 256), (FR, 128)], x, w)


def project_wires(z, x, w):
    return project(project_wires_kernel, 7 * FR, 384, [(7, FR * 3 // 2, 128)] * 2, z[None], x, w)


def project_own(x, w):
    return project(project_own_kernel, ROWS, 640, [(ROWS, 256), (ROWS, 128), (ROWS, 256)], x, w)


def attend_jobs(jobs, n, kid_ref, kv_ref, key_lane):
    scale = HEAD**-0.5 * 1.4426950408889634
    scores, tops, outs = [], [], []
    for q, qid, first in jobs:
        tiles, top = [], None
        for t in range(n):
            at = pl.multiple_of(first + t * TILE, 128)
            keys = kv_ref[pl.ds(at, TILE), key_lane : key_lane + 128]
            s = lax.dot_general(q, keys, (((1,), (1,)), ((), ())), preferred_element_type=jnp.float32)
            s = jnp.where(qid == kid_ref[:, pl.ds(at, TILE)], s, -1e30)
            tiles.append(s)
            most = jnp.maximum(s[:, :128], s[:, 128:])
            top = most if top is None else jnp.maximum(top, most)
        scores.append(tiles)
        tops.append(jnp.max(top, axis=1, keepdims=True))
    for (q, qid, first), tiles, top in zip(jobs, scores, tops):
        total = acc = None
        for t in range(n):
            at = pl.multiple_of(first + t * TILE, 128)
            p = jnp.exp2((tiles[t] - top) * scale)
            part_sum = p[:, :128] + p[:, 128:]
            out = jnp.dot(p.astype(jnp.bfloat16), kv_ref[pl.ds(at, TILE), :], preferred_element_type=jnp.float32)
            total = part_sum if total is None else total + part_sum
            acc = out if acc is None else acc + out
        outs.append(acc * (1.0 / jnp.sum(total, axis=1, keepdims=True)))
    return outs


def attend_kernel(head, group, info_ref, qid_ref, kid_ref, q_ref, *refs):
    *parts, out_ref, kv_ref = refs
    kv_ref[SEQ:, :] = jnp.zeros((TILE, 256), jnp.bfloat16)
    whole, shared = (slice(0, 128), slice(128, 256)) if head == 0 else (slice(128, 256), slice(0, 128))

    def keep(place, most, last, start):
        at, rows = (pl.ds(pl.multiple_of(i, FR), FR) for i in (place * FR, start))
        if head == 0:
            kv_ref[at, :] = most[rows, :]
        else:
            kv_ref[at, :128] = most[rows, 128:]
            kv_ref[at, 128:] = last[rows, :]

    wire_ref, most_ref, near_most_ref, last_ref, near_last_ref, packed_ref = parts if head else (*parts, None, None, None)
    for s in range(NZ):
        keep(info_ref[s], most_ref, last_ref, info_ref[40 + s] * FR)
    keep(info_ref[NZ + 7], near_most_ref, near_last_ref, 0)
    for s in range(7):
        place = info_ref[NZ + s] * FR
        packed = wire_ref[s, FR:, :]
        kv_ref[pl.ds(pl.multiple_of(place, FR), FR), whole] = wire_ref[s, :FR, :]
        kv_ref[pl.ds(pl.multiple_of(place, 96), 96), shared] = packed
        turned = pltpu.roll(packed.astype(jnp.float32), 64, 1).astype(jnp.bfloat16)
        kv_ref[pl.ds(pl.multiple_of(place + 96, 96), 96), shared] = turned

    def some(g, _):
        slots = [info_ref[32 + group * g + i] for i in range(group)]
        count = info_ref[24 + slots[-1]]
        jobs = []
        for s in slots:
            rows = pl.ds(pl.multiple_of(s * FR, FR), FR)
            query_rows = pl.ds(pl.multiple_of(info_ref[40 + s] * FR, FR), FR)
            first = jnp.minimum(info_ref[16 + s], PAD - count * TILE)
            jobs.append((q_ref[query_rows, head * 128 : head * 128 + 128], qid_ref[rows, :], first))

        def attend_some(n):
            outs = attend_jobs(jobs, n, kid_ref, kv_ref, head * 128)
            lane = lax.broadcasted_iota(jnp.int32, (FR, 128), 1)
            for s, acc in zip(slots, outs):
                z = info_ref[40 + s]
                if head == 0:
                    out_ref[z] = jnp.where(lane < 64, acc[:, 128:], acc[:, :128]).astype(jnp.bfloat16)
                    continue
                spare = (lane >= 64) & (lane < 96)
                first = jnp.where(spare, pltpu.roll(acc[:, 128:], 64, 1), packed_ref[z].astype(jnp.float32))
                out_ref[z, :FR, :] = first.astype(jnp.bfloat16)
                upper, lower = acc[: FR // 2, :128], acc[FR // 2 :, :128]
                both_rows = jnp.where(lane[: FR // 2] < 64, pltpu.roll(lower, 64, 1), upper)
                out_ref[z, FR:, :] = both_rows.astype(jnp.bfloat16)

        for n in range(1, MAX_TILES + 1):
            pl.when(count == n)(functools.partial(attend_some, n))
        return 0

    lax.fori_loop(0, NZ // group, some, 0)


def attend(head, info, qid, kid, *parts, group=2):
    return pl.pallas_call(
        functools.partial(attend_kernel, head, group),
        in_specs=[SMEM, VMEM, VMEM] + [VMEM] * len(parts),
        out_specs=VMEM,
        out_shape=jax.ShapeDtypeStruct((NZ, (FR, FR * 3 // 2)[head], 128), jnp.bfloat16),
        scratch_shapes=[pltpu.VMEM((PAD, 256), jnp.bfloat16)],
        compiler_params=pltpu.CompilerParams(vmem_limit_bytes=14 << 20),
        cost_estimate=pl.CostEstimate(flops=4 << 30, bytes_accessed=4 << 20, transcendentals=2 << 20),
    )(info, qid, kid, *parts)


def unpack_kernel(in_ref, out_ref):
    lane = lax.broadcasted_iota(jnp.int32, (FR, 128), 1)
    for z in range(0, NZ, 2):
        tiles = []
        for i in range(2):
            a = in_ref[z + i, :FR, :].astype(jnp.float32)
            b = in_ref[z + i, FR:, :].astype(jnp.float32)
            tiles.append((pltpu.roll(a, 32, 1), pltpu.roll(a, 96, 1)))
            tiles.append([jnp.concatenate([pltpu.roll(b, by, 1), pltpu.roll(b, by + 64, 1)], axis=0) for by in (32, 96)[i : i + 1]])
        (a32, a96), (b32,), (c32, c96), (d96,) = tiles
        out = (
            jnp.where(lane < 96, a32, b32),
            jnp.where(lane < 32, b32, jnp.where(lane < 64, a96, c96)),
            jnp.where(lane < 32, c96, jnp.where(lane < 96, d96, c32)),
        )
        for i, tile in enumerate(out):
            out_ref[:, z * 192 + i * 128 : z * 192 + (i + 1) * 128] = tile.astype(jnp.bfloat16)


def unpack(packed):
    return pl.pallas_call(
        unpack_kernel,
        in_specs=[VMEM],
        out_specs=VMEM,
        out_shape=jax.ShapeDtypeStruct((FR, D), jnp.bfloat16),
        compiler_params=pltpu.CompilerParams(vmem_limit_bytes=8 << 20),
    )(packed)


def plan(ids, order, z, xh):
    blocks = ids.reshape(16, FR)
    zs = (z + 1 + jnp.arange(NZ, dtype=jnp.int32)) % NZ
    places = jnp.take(order.reshape(NZ, 2), zs, axis=0)
    own = jnp.where(xh == 0, places[:, 0], places[:, 1])
    other = jnp.where(xh == 0, places[:, 1], places[:, 0])
    qid = jnp.take(blocks, own, axis=0)
    first = jnp.sum(ids[None, :] < qid[:, :1], axis=1, dtype=jnp.int32)
    last = jnp.sum(ids[None, :] <= qid[:, FR - 1 :], axis=1, dtype=jnp.int32)
    first = first // 128 * 128
    count = (last - first + TILE - 1) // TILE
    i = jnp.arange(NZ, dtype=jnp.int32)
    ahead = (count[None, :] < count[:, None]) | ((count[None, :] == count[:, None]) & (i[None, :] < i[:, None]))
    rank = jnp.sum(ahead, axis=1, dtype=jnp.int32)
    ranked = jnp.sum(jnp.where(rank[:, None] == i[None, :], i[:, None], 0), axis=0, dtype=jnp.int32)
    info = jnp.concatenate([own, other, first, count, ranked, zs])
    kid = jnp.concatenate([ids, jnp.full((TILE,), -1, jnp.int32)])[None]
    return info, qid.reshape(ROWS, 1), kid


def body(frames, seg_ids, assign, w_qkv):
    z, xh = lax.axis_index("z").astype(jnp.int32), lax.axis_index("xh")
    x = lax.all_gather(frames, "z", axis=0, tiled=True)
    w, partner = gather_weights(w_qkv, frames)
    near_most, near_last = project_near(partner, w)
    info, qid, kid = plan(seg_ids[0], assign[0], z, xh)
    x, info, qid, kid, near_last = lax.optimization_barrier((x, info, qid, kid, near_last))
    wire0, wire1 = project_wires(z, x, w)
    other0, other1 = swap(wire0, "xh"), swap(wire1, "xh")
    most, last, q = project_own(x, w)
    packed = attend(0, info, qid, kid, q, other0, most, near_most)
    packed = attend(1, info, qid, kid, q, other1, most, near_most, last, near_last, packed)
    return unpack(lax.all_to_all(packed, "z", 0, 0, tiled=True))


def solution(mesh):
    fine = Mesh(mesh.devices.reshape(SIZES), AXES)
    dp, ctx = AXES[:3], AXES[3:]
    return jax.shard_map(
        body,
        mesh=fine,
        in_specs=(P(AXES, None), P(dp, None), P(dp, None), P(None, dp, ctx)),
        out_specs=P(AXES, None),
        check_vma=False,
    )
```

```python
import functools

import jax
import jax.numpy as jnp
from jax import lax
from jax.experimental import pallas as pl
from jax.experimental.pallas import tpu as pltpu
from jax.sharding import Mesh
from jax.sharding import PartitionSpec as P

HEAD = 96
FR = 192
D = 1536
NZ = 8
ROWS = NZ * FR
SEQ = 3072
TILE = 256
MAX_TILES = 8
PAD = SEQ + TILE
AXES = ("y", "xl", "core", "z", "xh")
SIZES = (8, 2, 2, 8, 2)
VMEM = pl.BlockSpec(memory_space=pltpu.VMEM)
SMEM = pl.BlockSpec(memory_space=pltpu.SMEM)


def swap(x, axis):
    return lax.ppermute(x, axis, [(0, 1), (1, 0)])


def both(own, other, index, axis):
    first = jnp.where(index == 0, own, other)
    second = jnp.where(index == 0, other, own)
    return jnp.stack([first, second], axis=axis)


def gather_weights(w, frames):
    flat = jnp.transpose(w, (1, 0, 2)).reshape(w.shape[1], 3 * HEAD)
    heads = both(flat, swap(flat, "xh"), lax.axis_index("xh"), 0)
    q, k, v = (heads[:, :, t * HEAD : (t + 1) * HEAD] for t in range(3))
    shard = jnp.concatenate([k[0], v[0], v[1], k[1], q[0], jnp.zeros_like(q[0, :, :64]), q[1]], axis=1)
    frames, shard = lax.optimization_barrier((frames, shard))
    partner = swap(frames, "xh")
    rows = lax.all_to_all(jnp.broadcast_to(shard[None], (8,) + shard.shape), "y", 0, 0, tiled=True)
    rows, partner = lax.optimization_barrier((rows, partner))
    rows = both(rows, swap(rows, "xl"), lax.axis_index("xl"), 1)
    rows = both(rows, swap(rows, "core"), lax.axis_index("core"), 2)
    return rows.reshape(D, shard.shape[1]), partner


def project_near_kernel(x_ref, w_ref, most_ref, last_ref):
    y = jnp.dot(x_ref[...], w_ref[:, :384], preferred_element_type=jnp.float32).astype(jnp.bfloat16)
    most_ref[...] = y[:, :256]
    last_ref[...] = y[:, 256:]


def rotated(z_ref, x_ref, blocks):
    starts = [pl.multiple_of(lax.rem(z_ref[0] + 1 + i, NZ) * FR, FR) for i in range(blocks)]
    return jnp.concatenate([x_ref[pl.ds(start, FR), :] for start in starts], axis=0)


def project_wire_kernel(z_ref, x_ref, w_ref, wire_ref):
    y = jnp.dot(rotated(z_ref, x_ref, 7), w_ref[:, :256], preferred_element_type=jnp.float32)
    half = lax.broadcasted_iota(jnp.int32, (FR // 2, 128), 1) < 64
    for b in range(7):
        block = y[b * FR : (b + 1) * FR]
        wire_ref[b, :FR, :] = block[:, :128].astype(jnp.bfloat16)
        upper, turned = block[: FR // 2, 128:], pltpu.roll(block[FR // 2 :, 128:], 64, 1)
        wire_ref[b, FR:, :] = jnp.where(half, upper, turned).astype(jnp.bfloat16)


def project_own_kernel(z_ref, x_ref, w_ref, most_ref, last_ref, q_ref, wire_ref):
    y = jnp.dot(rotated(z_ref, x_ref, NZ), w_ref[...], preferred_element_type=jnp.float32)
    most_ref[...] = y[:, :256].astype(jnp.bfloat16)
    last_ref[...] = y[:, 256:384].astype(jnp.bfloat16)
    q_ref[...] = y[:, 384:].astype(jnp.bfloat16)
    half = lax.broadcasted_iota(jnp.int32, (FR // 2, 128), 1) < 64
    for b in range(7):
        block = y[b * FR : (b + 1) * FR]
        wire_ref[b, :FR, :] = block[:, 256:384].astype(jnp.bfloat16)
        upper, turned = block[: FR // 2, 128:256], pltpu.roll(block[FR // 2 :, 128:256], 64, 1)
        wire_ref[b, FR:, :] = jnp.where(half, turned, upper).astype(jnp.bfloat16)


def project(kernel, rows, columns, shapes, *args):
    return pl.pallas_call(
        kernel,
        in_specs=[SMEM] * (len(args) - 2) + [VMEM] * 2,
        out_specs=[VMEM] * len(shapes),
        out_shape=[jax.ShapeDtypeStruct(shape, jnp.bfloat16) for shape in shapes],
        compiler_params=pltpu.CompilerParams(vmem_limit_bytes=24 << 20),
        cost_estimate=pl.CostEstimate(
            flops=2 * rows * D * columns, bytes_accessed=rows * D * 4, transcendentals=0
        ),
    )(*args)


def project_near(x, w):
    return project(project_near_kernel, FR, 384, [(FR, 256), (FR, 128)], x, w)


def project_wire(z, x, w):
    return project(project_wire_kernel, 7 * FR, 256, [(7, FR * 3 // 2, 128)], z[None], x, w)[0]


def project_own(z, x, w):
    shapes = [(ROWS, 256), (ROWS, 128), (ROWS, 256), (7, FR * 3 // 2, 128)]
    return project(project_own_kernel, ROWS, 640, shapes, z[None], x, w)


def attend_jobs(jobs, n, kid_ref, kv_ref, key_lane):
    scale = HEAD**-0.5 * 1.4426950408889634
    scores, tops, outs = [], [], []
    for q, qid, first in jobs:
        tiles, top = [], None
        for t in range(n):
            at = pl.multiple_of(first + t * TILE, 128)
            keys = kv_ref[pl.ds(at, TILE), key_lane : key_lane + 128]
            s = lax.dot_general(q, keys, (((1,), (1,)), ((), ())), preferred_element_type=jnp.float32)
            s = jnp.where(qid == kid_ref[:, pl.ds(at, TILE)], s, -1e30)
            tiles.append(s)
            most = jnp.maximum(s[:, :128], s[:, 128:])
            top = most if top is None else jnp.maximum(top, most)
        scores.append(tiles)
        tops.append(jnp.max(top, axis=1, keepdims=True))
    for (q, qid, first), tiles, top in zip(jobs, scores, tops):
        total = acc = None
        for t in range(n):
            at = pl.multiple_of(first + t * TILE, 128)
            p = jnp.exp2((tiles[t] - top) * scale)
            part_sum = p[:, :128] + p[:, 128:]
            out = jnp.dot(p.astype(jnp.bfloat16), kv_ref[pl.ds(at, TILE), :], preferred_element_type=jnp.float32)
            total = part_sum if total is None else total + part_sum
            acc = out if acc is None else acc + out
        outs.append(acc * (1.0 / jnp.sum(total, axis=1, keepdims=True)))
    return outs


def attend_kernel(head, group, info_ref, qid_ref, kid_ref, q_ref, *refs):
    *parts, out_ref, kv_ref = refs
    kv_ref[SEQ:, :] = jnp.zeros((TILE, 256), jnp.bfloat16)
    whole, shared = (slice(0, 128), slice(128, 256)) if head == 0 else (slice(128, 256), slice(0, 128))

    def keep(place, most, last, start):
        at, rows = (pl.ds(pl.multiple_of(i, FR), FR) for i in (place * FR, start))
        if head == 0:
            kv_ref[at, :] = most[rows, :]
        else:
            kv_ref[at, :128] = most[rows, 128:]
            kv_ref[at, 128:] = last[rows, :]

    wire_ref, most_ref, near_most_ref, last_ref, near_last_ref, packed_ref = parts if head else (*parts, None, None, None)
    for s in range(NZ):
        keep(info_ref[s], most_ref, last_ref, s * FR)
    keep(info_ref[NZ + 7], near_most_ref, near_last_ref, 0)
    for s in range(7):
        place = info_ref[NZ + s] * FR
        packed = wire_ref[s, FR:, :]
        kv_ref[pl.ds(pl.multiple_of(place, FR), FR), whole] = wire_ref[s, :FR, :]
        kv_ref[pl.ds(pl.multiple_of(place, 96), 96), shared] = packed
        turned = pltpu.roll(packed.astype(jnp.float32), 64, 1).astype(jnp.bfloat16)
        kv_ref[pl.ds(pl.multiple_of(place + 96, 96), 96), shared] = turned

    def some(g, _):
        slots = [info_ref[32 + group * g + i] for i in range(group)]
        count = info_ref[24 + slots[-1]]
        jobs = []
        for s in slots:
            rows = pl.ds(pl.multiple_of(s * FR, FR), FR)
            first = jnp.minimum(info_ref[16 + s], PAD - count * TILE)
            jobs.append((q_ref[rows, head * 128 : head * 128 + 128], qid_ref[rows, :], first))

        def attend_some(n):
            outs = attend_jobs(jobs, n, kid_ref, kv_ref, head * 128)
            lane = lax.broadcasted_iota(jnp.int32, (FR, 128), 1)
            for s, acc in zip(slots, outs):
                z = info_ref[40 + s]
                if head == 0:
                    out_ref[z] = jnp.where(lane < 64, acc[:, 128:], acc[:, :128]).astype(jnp.bfloat16)
                    continue
                spare = (lane >= 64) & (lane < 96)
                first = jnp.where(spare, pltpu.roll(acc[:, 128:], 64, 1), packed_ref[z].astype(jnp.float32))
                out_ref[z, :FR, :] = first.astype(jnp.bfloat16)
                upper, lower = acc[: FR // 2, :128], acc[FR // 2 :, :128]
                both_rows = jnp.where(lane[: FR // 2] < 64, pltpu.roll(lower, 64, 1), upper)
                out_ref[z, FR:, :] = both_rows.astype(jnp.bfloat16)

        for n in range(1, MAX_TILES + 1):
            pl.when(count == n)(functools.partial(attend_some, n))
        return 0

    lax.fori_loop(0, NZ // group, some, 0)


def attend(head, info, qid, kid, *parts, group=2):
    return pl.pallas_call(
        functools.partial(attend_kernel, head, group),
        in_specs=[SMEM, VMEM, VMEM] + [VMEM] * len(parts),
        out_specs=VMEM,
        out_shape=jax.ShapeDtypeStruct((NZ, (FR, FR * 3 // 2)[head], 128), jnp.bfloat16),
        scratch_shapes=[pltpu.VMEM((PAD, 256), jnp.bfloat16)],
        compiler_params=pltpu.CompilerParams(vmem_limit_bytes=14 << 20),
        cost_estimate=pl.CostEstimate(flops=4 << 30, bytes_accessed=4 << 20, transcendentals=2 << 20),
    )(info, qid, kid, *parts)


def unpack_kernel(in_ref, out_ref):
    lane = lax.broadcasted_iota(jnp.int32, (FR, 128), 1)
    for z in range(0, NZ, 2):
        tiles = []
        for i in range(2):
            a = in_ref[z + i, :FR, :].astype(jnp.float32)
            b = in_ref[z + i, FR:, :].astype(jnp.float32)
            tiles.append((pltpu.roll(a, 32, 1), pltpu.roll(a, 96, 1)))
            tiles.append([jnp.concatenate([pltpu.roll(b, by, 1), pltpu.roll(b, by + 64, 1)], axis=0) for by in (32, 96)[i : i + 1]])
        (a32, a96), (b32,), (c32, c96), (d96,) = tiles
        out = (
            jnp.where(lane < 96, a32, b32),
            jnp.where(lane < 32, b32, jnp.where(lane < 64, a96, c96)),
            jnp.where(lane < 32, c96, jnp.where(lane < 96, d96, c32)),
        )
        for i, tile in enumerate(out):
            out_ref[:, z * 192 + i * 128 : z * 192 + (i + 1) * 128] = tile.astype(jnp.bfloat16)


def unpack(packed):
    return pl.pallas_call(
        unpack_kernel,
        in_specs=[VMEM],
        out_specs=VMEM,
        out_shape=jax.ShapeDtypeStruct((FR, D), jnp.bfloat16),
        compiler_params=pltpu.CompilerParams(vmem_limit_bytes=8 << 20),
    )(packed)


def plan(ids, order, z, xh):
    blocks = ids.reshape(16, FR)
    zs = (z + 1 + jnp.arange(NZ, dtype=jnp.int32)) % NZ
    places = jnp.take(order.reshape(NZ, 2), zs, axis=0)
    own = jnp.where(xh == 0, places[:, 0], places[:, 1])
    other = jnp.where(xh == 0, places[:, 1], places[:, 0])
    qid = jnp.take(blocks, own, axis=0)
    first = jnp.sum(ids[None, :] < qid[:, :1], axis=1, dtype=jnp.int32)
    last = jnp.sum(ids[None, :] <= qid[:, FR - 1 :], axis=1, dtype=jnp.int32)
    first = first // 128 * 128
    count = (last - first + TILE - 1) // TILE
    i = jnp.arange(NZ, dtype=jnp.int32)
    ahead = (count[None, :] < count[:, None]) | ((count[None, :] == count[:, None]) & (i[None, :] < i[:, None]))
    rank = jnp.sum(ahead, axis=1, dtype=jnp.int32)
    ranked = jnp.sum(jnp.where(rank[:, None] == i[None, :], i[:, None], 0), axis=0, dtype=jnp.int32)
    info = jnp.concatenate([own, other, first, count, ranked, zs])
    kid = jnp.concatenate([ids, jnp.full((TILE,), -1, jnp.int32)])[None]
    return info, qid.reshape(ROWS, 1), kid


def body(frames, seg_ids, assign, w_qkv):
    z, xh = lax.axis_index("z").astype(jnp.int32), lax.axis_index("xh")
    x = lax.all_gather(frames, "z", axis=0, tiled=True)
    w, partner = gather_weights(w_qkv, frames)
    near_most, near_last = project_near(partner, w)
    info, qid, kid = plan(seg_ids[0], assign[0], z, xh)
    x, info, qid, kid, near_last = lax.optimization_barrier((x, info, qid, kid, near_last))
    other0 = swap(project_wire(z, x, w), "xh")
    most, last, q, wire1 = project_own(z, x, w)
    other1 = swap(wire1, "xh")
    packed = attend(0, info, qid, kid, q, other0, most, near_most)
    packed = attend(1, info, qid, kid, q, other1, most, near_most, last, near_last, packed)
    return unpack(lax.all_to_all(packed, "z", 0, 0, tiled=True))


def solution(mesh):
    fine = Mesh(mesh.devices.reshape(SIZES), AXES)
    dp, ctx = AXES[:3], AXES[3:]
    return jax.shard_map(
        body,
        mesh=fine,
        in_specs=(P(AXES, None), P(dp, None), P(dp, None), P(None, dp, ctx)),
        out_specs=P(AXES, None),
        check_vma=False,
    )
```
